32 devices in a mesh: seq: 8 (over y, x, core), ch: 4 (over z).
Axes of the slice: x: 2, y: 2, z: 4, core: 2. Of those that a mesh axis runs over, the one named last changes fastest.
Arguments:
- grad_out: bfloat16 [1024, 8192], P('seq', 'ch'), may hold values from -6 to 6
- out_weight: bfloat16 [8192, 8192], P('ch'), may hold values from -0.0625 to 0.0625
- query_gate: bfloat16 [1024, 8192], P('seq', 'ch'), may hold values from -6 to 6
- key_branch: bfloat16 [1024, 8192], P('seq', 'ch'), may hold values from -6 to 6
- value_branch: bfloat16 [1024, 8192], P('seq', 'ch'), may hold values from -6 to 6
- filter_taps: bfloat16 [1024, 8192], P('seq', 'ch'), may hold values from -4 to 4
Outputs:
- key_grad: bfloat16 [1024, 8192], P('seq', 'ch')
- value_grad: bfloat16 [1024, 8192], P('seq', 'ch')
- filter_grad: float32 [1024, 8192], P('seq', 'ch')
The draws below stay inside these ranges and needn't reach their ends.
All inputs are finite; a program needn't handle non-finite values.
Results may differ from the reference program's by a relative error of at most 0.017.
Values may be sent and summed in bfloat16 or wider, within the bound.
No kernel may reach another device: no remote copies, remote signals or barrier semaphores. Data moves between devices by JAX's collectives and lax.ppermute only.
A program may use at most 192 MiB of HBM per device.

```python
import math
import jax
import jax.numpy as jnp
from jax import lax

D = 8192
LS = 128
SEQ = 1024
N_SEQ = 8


def draw_filter_taps(key, part):
    rate_key, noise_key = jax.random.split(jax.random.fold_in(key, 17))
    fraction = jax.random.uniform(rate_key, (1, D), jnp.float32)
    lag_index = jnp.arange(SEQ, dtype=jnp.float32)[:, None]
    log_low = math.log(LS / 4.0)
    log_high = math.log(2.0 * SEQ)
    noise_part = jnp.clip(jax.random.normal(noise_key, (SEQ, D), jnp.float32), -4.0, 4.0)
    reach_len = jnp.exp(log_low + fraction * (log_high - log_low))
    return (noise_part * jnp.sqrt(2.0 / reach_len) * jnp.exp(-lag_index / reach_len)).astype(jnp.bfloat16)


def block_scale(stream_key, extent, pieces, low, high):
    factor_of = 1.0
    for axis_at, blocks in pieces:
        steps = jax.random.uniform(jax.random.fold_in(jax.random.fold_in(stream_key, 6), axis_at), (blocks,), jnp.float32, low / len(pieces), high / len(pieces))
        factor_of = factor_of * jnp.repeat(jnp.exp(steps), extent[axis_at] // blocks).reshape((-1,) + (1,) * (len(extent) - 1 - axis_at))
    return factor_of


def scatter_about(stream_key, shape, width, most, pieces=(), held_as=jnp.bfloat16):
    level = block_scale(stream_key, shape, pieces, -0.22, 0.18) if pieces else 1.0
    drawn = jax.random.normal(stream_key, shape, jnp.float32) * width * level
    return jnp.minimum(jnp.maximum(drawn, -most), most).astype(held_as)


def setup_inputs(seed: int = 0) -> dict:
    key_of = jax.random.split(jax.random.key(seed), 7)
    return {
        "grad_out": scatter_about(key_of[0], (SEQ, D), 1.0, 6.0, ((0, 8), (1, 4))),
        "out_weight": scatter_about(key_of[1], (D, D), D ** -0.5, 0.0625, ((0, 4),)),
        "query_gate": scatter_about(key_of[2], (SEQ, D), 1.0, 6.0, ((0, 8), (1, 4))),
        "key_branch": scatter_about(key_of[3], (SEQ, D), 1.0, 6.0, ((0, 8), (1, 4))),
        "value_branch": scatter_about(key_of[4], (SEQ, D), 1.0, 6.0, ((0, 8), (1, 4))),
        "filter_taps": draw_filter_taps(jax.random.fold_in(key_of[6], 71), 0),
    }


def build_tables(seg_len):
    twice_length = 2 * seg_len
    freq_index = jnp.arange(twice_length, dtype=jnp.int32)
    row_index = jnp.arange(seg_len, dtype=jnp.int32)
    angle_unit = 2.0 * math.pi / twice_length
    fwd_phase = (freq_index[:, None] * row_index[None, :] % twice_length).astype(jnp.float32) * angle_unit
    back_phase = (freq_index[None, :] * (seg_len - row_index[:, None]) % twice_length).astype(jnp.float32) * angle_unit
    window_pos = (freq_index + seg_len) % twice_length
    window_phase = (freq_index[None, :] * window_pos[:, None] % twice_length).astype(jnp.float32) * angle_unit
    parity = jnp.where(freq_index % 2 == 0, 1.0, -1.0).astype(jnp.float32)[:, None]
    return (jnp.cos(fwd_phase).astype(jnp.bfloat16), jnp.sin(fwd_phase).astype(jnp.bfloat16), jnp.cos(back_phase).astype(jnp.bfloat16), jnp.sin(back_phase).astype(jnp.bfloat16), jnp.cos(window_phase).astype(jnp.bfloat16), jnp.sin(window_phase).astype(jnp.bfloat16), parity)

def transform_roundtrip(values):
    rounded = lax.optimization_barrier(values.astype(jnp.bfloat16))
    return rounded.astype(jnp.float32)

def reference(grad_out, out_weight, query_gate, key_branch, value_branch, filter_taps):
    twice_length = 2 * LS
    highest_precision = lax.Precision.HIGHEST
    grad_mix = jnp.dot(grad_out, out_weight.T, preferred_element_type=jnp.float32)
    gated_grad = (grad_mix * query_gate.astype(jnp.float32)).astype(jnp.bfloat16)
    conv_input = (key_branch.astype(jnp.float32) * value_branch.astype(jnp.float32)).astype(jnp.bfloat16)
    cosine_forward, sine_forward, cosine_backward, sine_backward, cosine_window, sine_window, parity = build_tables(LS)

    def spectra(whole):
        block_list = whole.astype(jnp.float32).reshape(N_SEQ, LS, D)
        cosine_piece = jnp.einsum('qk,rkb->rqb', cosine_forward.astype(jnp.float32), block_list, precision=highest_precision)
        sine_piece = jnp.einsum('qk,rkb->rqb', sine_forward.astype(jnp.float32), block_list, precision=highest_precision)
        return (cosine_piece, sine_piece)
    grad_cos, grad_sin = spectra(gated_grad)
    conv_cos, conv_sin = spectra(conv_input)
    tap_cos, tap_sin = spectra(filter_taps)
    kern_cos = jnp.concatenate([jnp.zeros_like(tap_cos[:1]), tap_cos[:-1]], 0) + parity * tap_cos
    kern_sin = jnp.concatenate([jnp.zeros_like(tap_sin[:1]), tap_sin[:-1]], 0) + parity * tap_sin

    def shifted_spec(spec, offset):
        return jnp.concatenate([spec[offset:], jnp.zeros_like(spec[:offset])], 0)
    running_real = jnp.zeros_like(grad_cos)
    running_imaginary = jnp.zeros_like(grad_cos)
    windows = []
    for offset in range(N_SEQ):
        later_cos = shifted_spec(grad_cos, offset)
        later_sin = shifted_spec(grad_sin, offset)
        running_real = running_real + later_cos * kern_cos[offset] + later_sin * kern_sin[offset]
        running_imaginary = running_imaginary + later_sin * kern_cos[offset] - later_cos * kern_sin[offset]
        product_real = transform_roundtrip(conv_cos * later_cos + conv_sin * later_sin)
        product_imaginary = transform_roundtrip(conv_sin * later_cos - conv_cos * later_sin)
        real_total = lax.optimization_barrier(jnp.sum(product_real, axis=0))
        imag_total = lax.optimization_barrier(jnp.sum(product_imaginary, axis=0))
        window = (jnp.dot(cosine_window.astype(jnp.float32), real_total, precision=highest_precision) - jnp.dot(sine_window.astype(jnp.float32), imag_total, precision=highest_precision)) / twice_length
        windows.append(window)
    convolution_gradient = (jnp.einsum('ux,axo->auo', cosine_backward.astype(jnp.float32), transform_roundtrip(running_real), precision=highest_precision) - jnp.einsum('ux,axo->auo', sine_backward.astype(jnp.float32), transform_roundtrip(running_imaginary), precision=highest_precision)) / twice_length
    convolution_gradient = convolution_gradient.reshape(SEQ, D)
    key_grad = (convolution_gradient * value_branch.astype(jnp.float32)).astype(jnp.bfloat16)
    value_grad = (convolution_gradient * key_branch.astype(jnp.float32)).astype(jnp.bfloat16)
    lag_blocks = []
    for offset in range(N_SEQ):
        block_sum = windows[offset][LS:]
        if offset + 1 < N_SEQ:
            block_sum = block_sum + windows[offset + 1][:LS]
        lag_blocks.append(block_sum)
    lag_grad = jnp.concatenate(lag_blocks, 0)
    filter_grad = lag_grad * (1.0 / math.sqrt(SEQ))
    return (key_grad, value_grad, filter_grad)
```

```python
import functools
import math

import jax
import jax.numpy as jnp
import ml_dtypes
import numpy as np
from jax import lax
from jax.experimental import pallas as pl
from jax.experimental.pallas import tpu as pltpu
from jax.sharding import PartitionSpec as P

LANES = 128
CHUNKS = 2


def build_tables(seg_len):
    twice_length = 2 * seg_len
    freq_index = jnp.arange(twice_length, dtype=jnp.int32)
    row_index = jnp.arange(seg_len, dtype=jnp.int32)
    angle_unit = 2.0 * math.pi / twice_length
    fwd_phase = (freq_index[:, None] * row_index[None, :] % twice_length).astype(
        jnp.float32
    ) * angle_unit
    back_phase = (freq_index[None, :] * (seg_len - row_index[:, None]) % twice_length).astype(
        jnp.float32
    ) * angle_unit
    window_pos = (freq_index + seg_len) % twice_length
    window_phase = (freq_index[None, :] * window_pos[:, None] % twice_length).astype(
        jnp.float32
    ) * angle_unit
    parity = jnp.where(freq_index % 2 == 0, 1.0, -1.0).astype(jnp.float32)[:, None]
    return (
        jnp.cos(fwd_phase).astype(jnp.bfloat16),
        jnp.sin(fwd_phase).astype(jnp.bfloat16),
        jnp.cos(back_phase).astype(jnp.bfloat16),
        jnp.sin(back_phase).astype(jnp.bfloat16),
        jnp.cos(window_phase).astype(jnp.bfloat16),
        jnp.sin(window_phase).astype(jnp.bfloat16),
        parity,
    )


def spectra(block_list, cosine_forward, sine_forward):
    cosine_piece = jnp.einsum(
        "qk,rkb->rqb", cosine_forward, block_list, preferred_element_type=jnp.float32
    )
    sine_piece = jnp.einsum(
        "qk,rkb->rqb", sine_forward, block_list, preferred_element_type=jnp.float32
    )
    return (cosine_piece, sine_piece)


def shards(grad_out, out_weight, query_gate, key_branch, value_branch, filter_taps):
    seg_len = query_gate.shape[0]
    channels = query_gate.shape[1]
    twice_length = 2 * seg_len
    segments = lax.axis_size("seq")
    my_index = lax.axis_index("seq")
    factor = 1.0 / math.sqrt(seg_len * segments)
    grad_mix = lax.dot_general(
        lax.all_gather(grad_out, "ch", axis=1, tiled=True),
        out_weight,
        (((1,), (1,)), ((), ())),
        preferred_element_type=jnp.float32,
    )
    gated_grad = (grad_mix * query_gate.astype(jnp.float32)).astype(jnp.bfloat16)
    conv_input = (key_branch.astype(jnp.float32) * value_branch.astype(jnp.float32)).astype(
        jnp.bfloat16
    )
    tables = build_tables(seg_len)
    (
        cosine_forward,
        sine_forward,
        cosine_backward,
        sine_backward,
        cosine_window,
        sine_window,
        parity,
    ) = tables
    all_taps = lax.all_gather(filter_taps, "seq", axis=0, tiled=True)
    tap_cos, tap_sin = spectra(
        all_taps.reshape(segments, seg_len, channels), cosine_forward, sine_forward
    )
    kern_cos = jnp.concatenate([jnp.zeros_like(tap_cos[:1]), tap_cos[:-1]], 0) + parity * tap_cos
    kern_sin = jnp.concatenate([jnp.zeros_like(tap_sin[:1]), tap_sin[:-1]], 0) + parity * tap_sin
    own_cos, own_sin = spectra(conv_input[None], cosine_forward, sine_forward)
    own_cos = own_cos[0]
    own_sin = own_sin[0]
    zero_spec = jnp.zeros((twice_length, channels), jnp.float32)
    initial = (zero_spec, zero_spec, jnp.zeros(((segments + 1) * seg_len, channels), jnp.float32))
    piece_data = lax.all_gather(gated_grad, "seq", axis=0, tiled=True)
    block_count = piece_data.shape[0] // seg_len
    seg_ids = jnp.arange(block_count, dtype=jnp.int32)
    block_list = piece_data.reshape(block_count, seg_len, channels)
    grad_cos, grad_sin = spectra(block_list, cosine_forward, sine_forward)
    lag_steps = seg_ids - my_index
    inside = seg_ids < segments
    live_mask = ((lag_steps >= 0) & inside).astype(jnp.float32)[:, None, None]
    lag_clip = jnp.clip(lag_steps, 0, segments - 1)
    lag_kcos = jnp.take(kern_cos, lag_clip, axis=0)
    lag_ksin = jnp.take(kern_sin, lag_clip, axis=0)
    running_real = jnp.sum(live_mask * (grad_cos * lag_kcos + grad_sin * lag_ksin), axis=0)
    running_imaginary = jnp.sum(live_mask * (grad_sin * lag_kcos - grad_cos * lag_ksin), axis=0)
    product_real = (own_cos * grad_cos + own_sin * grad_sin).astype(jnp.bfloat16)
    product_imaginary = (own_sin * grad_cos - own_cos * grad_sin).astype(jnp.bfloat16)
    windows = jnp.einsum(
        "an,hny->hay", cosine_window, product_real, preferred_element_type=jnp.float32
    ) - jnp.einsum(
        "an,hny->hay", sine_window, product_imaginary, preferred_element_type=jnp.float32
    )
    windows = windows * (live_mask / twice_length)

    def place(item_index, buffer):
        offset = lag_clip[item_index] * seg_len
        current = lax.dynamic_slice_in_dim(buffer, offset, twice_length, 0)
        return lax.dynamic_update_slice_in_dim(buffer, current + windows[item_index], offset, 0)

    buffer = lax.fori_loop(0, block_list.shape[0], place, initial[2])
    convolution_gradient = (
        jnp.dot(
            cosine_backward, running_real.astype(jnp.bfloat16), preferred_element_type=jnp.float32
        )
        - jnp.dot(
            sine_backward,
            running_imaginary.astype(jnp.bfloat16),
            preferred_element_type=jnp.float32,
        )
    ) / twice_length
    own_rows = lax.psum_scatter(
        buffer[seg_len:].astype(jnp.bfloat16), "seq", scatter_dimension=0, tiled=True
    ).astype(jnp.float32)
    filter_grad = own_rows * factor
    key_grad = (convolution_gradient * value_branch.astype(jnp.float32)).astype(jnp.bfloat16)
    value_grad = (convolution_gradient * key_branch.astype(jnp.float32)).astype(jnp.bfloat16)
    return (key_grad, value_grad, filter_grad)


def half_tables(rows):
    size = 2 * rows
    freq = np.arange(rows)
    pos = np.arange(rows)
    angle = 2.0 * np.pi * (np.outer(freq, pos) % size) / size
    sine = np.sin(angle)
    sine[0] = (-1.0) ** pos
    forward = np.concatenate([np.cos(angle), sine], 0)
    angle = 2.0 * np.pi * (np.outer(rows - pos, freq) % size) / size
    cos_back = 2.0 * np.cos(angle)
    sin_back = -2.0 * np.sin(angle)
    cos_back[:, 0] = 1.0
    sin_back[:, 0] = (-1.0) ** (rows - pos)
    back = np.concatenate([cos_back, sin_back], 1) / size
    return forward.astype(ml_dtypes.bfloat16), back.astype(ml_dtypes.bfloat16)


def whole(shape):
    return pl.BlockSpec(shape, lambda *_: (0,) * len(shape))


def params(mib=48):
    return pltpu.CompilerParams(vmem_limit_bytes=mib * 2**20)


def pack_kernel(ids, key, value, taps, *outs):
    step = pl.program_id(0)
    conv_input = (key[...].astype(jnp.float32) * value[...].astype(jnp.float32)).astype(jnp.bfloat16)
    for k, out in enumerate(outs):

        @pl.when(step == k)
        def _():
            out[0] = taps[...]
            out[1] = conv_input


def pack(ids, key, value, taps, n):
    rows, channels = key.shape
    width = channels // n
    column = pl.BlockSpec((rows, width), lambda k, ids: (0, ids[0] ^ k))
    return pl.pallas_call(
        pack_kernel,
        grid_spec=pltpu.PrefetchScalarGridSpec(
            num_scalar_prefetch=1,
            grid=(n,),
            in_specs=[column] * 3,
            out_specs=[whole((2, rows, width))] * n,
        ),
        out_shape=[jax.ShapeDtypeStruct((2, rows, width), jnp.bfloat16)] * n,
        compiler_params=params(),
        name="pack_taps_input",
    )(ids, key, value, taps)


def contract(x, w):
    return lax.dot_general(x, w, (((1,), (1,)), ((), ())), preferred_element_type=jnp.float32)


def choose(ids, pair):
    if len(pair) == 1:
        return pair[0][...]
    return jnp.where(ids[2] == 1, pair[0][...], pair[1][...])


def mix_kernel(parts, per_part, has_total, ids, *refs):
    xs = refs[: parts * per_part]
    w, *rest = refs[parts * per_part :]
    total, out = rest if has_total else (None, rest[0])
    rows = xs[0].shape[0]
    for c in range(parts):
        block = contract(choose(ids, xs[c * per_part : (c + 1) * per_part]), w[...])
        if has_total:
            block += total[c * rows : (c + 1) * rows]
        out[c * rows : (c + 1) * rows] = block


def mix(ids, where, parts, weight, total, n):
    channels = weight.shape[0]
    depth = parts[0][0].shape[1]
    rows = sum(p[0].shape[0] for p in parts)
    width = channels // n
    flat = [x for p in parts for x in p]
    column = pl.BlockSpec((rows, width), lambda k, ids: (0, k))
    return pl.pallas_call(
        functools.partial(mix_kernel, len(parts), len(parts[0]), total is not None),
        grid_spec=pltpu.PrefetchScalarGridSpec(
            num_scalar_prefetch=1,
            grid=(n,),
            in_specs=[whole(x.shape) for x in flat]
            + [pl.BlockSpec((width, depth), lambda k, ids: (k, ids[where]))]
            + ([column] if total is not None else []),
            out_specs=column,
        ),
        out_shape=jax.ShapeDtypeStruct((rows, channels), jnp.float32),
        compiler_params=params(),
        name="mix",
    )(ids, *flat, weight, *([total] if total is not None else []))


def gate_kernel(per_part, ids, *refs):
    xs = refs[:per_part]
    w, total, gate, *outs = refs[per_part:]
    step = pl.program_id(0)
    mixed = total[...] + contract(choose(ids, xs), w[...])
    gated = (mixed * gate[...].astype(jnp.float32)).astype(jnp.bfloat16)
    for k, out in enumerate(outs):

        @pl.when(step == k)
        def _():
            out[...] = gated


def mix_gate(ids, where, pair, weight, total, gate, chunk, n):
    channels = weight.shape[0]
    rows, depth = pair[0].shape
    width = channels // n
    column = pl.BlockSpec((rows, width), lambda k, ids: (chunk, ids[0] ^ k))
    return pl.pallas_call(
        functools.partial(gate_kernel, len(pair)),
        grid_spec=pltpu.PrefetchScalarGridSpec(
            num_scalar_prefetch=1,
            grid=(n,),
            in_specs=[whole(x.shape) for x in pair]
            + [pl.BlockSpec((width, depth), lambda k, ids: (ids[0] ^ k, ids[where])), column, column],
            out_specs=[whole((rows, width))] * n,
        ),
        out_shape=[jax.ShapeDtypeStruct((rows, width), jnp.bfloat16)] * n,
        compiler_params=params(),
        name="mix_gate",
    )(ids, *pair, weight, total, gate)


def tap_kernel(n, ids, forward, *refs):
    pieces = refs[:n]
    out, data, spec = refs[n:]
    rows = pieces[0].shape[1]
    seg = forward.shape[1]
    for k in range(n):
        at = pl.multiple_of((ids[0] ^ k) * rows, rows)
        data[:, pl.ds(at, rows)] = pieces[k][...]
    row = lax.broadcasted_iota(jnp.int32, (2 * seg, data.shape[2]), 0)
    sign = jnp.where(row % 2 == 0, 1.0, -1.0)
    for x in range(2):
        for r in range(n * rows // seg):
            now = jnp.dot(forward[...], data[x, r * seg : (r + 1) * seg], preferred_element_type=jnp.float32)
            kern = sign * now
            if r:
                kern += spec[...]
            spec[...] = now
            out[x, r] = kern.astype(jnp.bfloat16)


def tap_kernels(ids, forward, pieces):
    n = len(pieces)
    _, rows, width = pieces[0].shape
    seg = forward.shape[1]
    shape = (2, n * rows // seg, 2 * seg, width)
    return pl.pallas_call(
        functools.partial(tap_kernel, n),
        grid_spec=pltpu.PrefetchScalarGridSpec(
            num_scalar_prefetch=1,
            grid=(1,),
            in_specs=[whole(forward.shape)] + [whole(p.shape) for p in pieces],
            out_specs=whole(shape),
            scratch_shapes=[
                pltpu.VMEM((2, n * rows, width), jnp.bfloat16),
                pltpu.VMEM((2 * seg, width), jnp.float32),
            ],
        ),
        out_shape=jax.ShapeDtypeStruct(shape, jnp.bfloat16),
        compiler_params=params(),
        name="kernels",
    )(ids, forward, *pieces)


def correlate_kernel(n, parts, ids, forward, back, kern, *refs):
    pieces = refs[: n * parts]
    outs = refs[n * parts : n * parts + n]
    data, spec, acc, result = refs[n * parts + n :]
    part_rows = pieces[0].shape[0]
    rows = part_rows * parts
    seg = forward.shape[1]
    segs = n * rows // seg
    width = data.shape[1]
    for k in range(n):
        for c in range(parts):
            at = pl.multiple_of((ids[0] ^ k) * rows + c * part_rows, part_rows)
            data[pl.ds(at, part_rows)] = pieces[k * parts + c][...]
    for i in range(segs):
        spec[i] = jnp.dot(forward[...], data[i * seg : (i + 1) * seg], preferred_element_type=jnp.float32)

    tile = 16

    def products(x, row, lane, first):
        here = (pl.ds(row, tile), pl.ds(lane, LANES))
        there = (pl.ds(row + seg, tile), pl.ds(lane, LANES))
        g_real = [spec[(i, *here)] for i in range(segs)]
        g_imag = [spec[(i, *there)] for i in range(segs)]
        k_real = [kern[(x, r, *here)].astype(jnp.float32) for r in range(segs)]
        k_imag = [kern[(x, r, *there)].astype(jnp.float32) for r in range(segs)]
        if first:
            edge = lax.broadcasted_iota(jnp.int32, (tile, LANES), 0) == 0
        for j in range(segs):
            both = sum(g_real[i] * k_real[i - j] for i in range(j, segs))
            other = sum(g_imag[i] * k_imag[i - j] for i in range(j, segs))
            cross = sum(g_imag[i] * k_real[i - j] - g_real[i] * k_imag[i - j] for i in range(j, segs))
            if first:
                real = both + jnp.where(edge, 0.0, other)
                cross = jnp.where(edge, other, cross)
            else:
                real = both + other
            acc[(j, *here)] = real.astype(jnp.bfloat16)
            acc[(j, *there)] = cross.astype(jnp.bfloat16)

    for x in range(2):
        for lane in range(0, width, LANES):
            products(x, 0, lane, True)

            @pl.loop(1, seg // tile)
            def _(t):
                products(x, pl.multiple_of(t * tile, tile), lane, False)

        for j in range(segs):
            value = jnp.dot(back[...], acc[j], preferred_element_type=jnp.float32).astype(jnp.bfloat16)
            for h in range(seg // rows):
                result[j * (seg // rows) + h, x] = value[h * rows : (h + 1) * rows]
    for k in range(n):
        outs[k][...] = result[ids[0] ^ k]


def correlate(ids, forward, back, kern, pieces):
    n, parts = len(pieces), len(pieces[0])
    flat = [p for group in pieces for p in group]
    part_rows, width = flat[0].shape
    rows = part_rows * parts
    seg = forward.shape[1]
    segs = n * rows // seg
    out = (2, rows, width)
    return pl.pallas_call(
        functools.partial(correlate_kernel, n, parts),
        grid_spec=pltpu.PrefetchScalarGridSpec(
            num_scalar_prefetch=1,
            grid=(1,),
            in_specs=[whole(a.shape) for a in (forward, back, kern, *flat)],
            out_specs=[whole(out)] * n,
            scratch_shapes=[
                pltpu.VMEM((n * rows, width), jnp.bfloat16),
                pltpu.VMEM((segs, 2 * seg, width), jnp.float32),
                pltpu.VMEM((segs, 2 * seg, width), jnp.bfloat16),
                pltpu.VMEM((n, *out), jnp.bfloat16),
            ],
        ),
        out_shape=[jax.ShapeDtypeStruct(out, jnp.bfloat16)] * n,
        compiler_params=params(),
        name="correlate",
    )(ids, forward, back, kern, *flat)


def finish_kernel(n, factor, ids, key, value, *refs):
    pieces = refs[:n]
    key_grad, value_grad, filter_grad = refs[n:]
    step = pl.program_id(0)
    for k in range(n):

        @pl.when(step == k)
        def _():
            conv_grad = pieces[k][0].astype(jnp.float32)
            key_grad[...] = (conv_grad * value[...].astype(jnp.float32)).astype(jnp.bfloat16)
            value_grad[...] = (conv_grad * key[...].astype(jnp.float32)).astype(jnp.bfloat16)
            filter_grad[...] = pieces[k][1].astype(jnp.float32) * factor


def finish(ids, key, value, pieces, factor):
    n = len(pieces)
    rows, channels = key.shape
    column = pl.BlockSpec((rows, channels // n), lambda k, ids: (0, ids[0] ^ k))
    return pl.pallas_call(
        functools.partial(finish_kernel, n, factor),
        grid_spec=pltpu.PrefetchScalarGridSpec(
            num_scalar_prefetch=1,
            grid=(n,),
            in_specs=[column] * 2 + [whole(p.shape) for p in pieces],
            out_specs=[column] * 3,
        ),
        out_shape=[
            jax.ShapeDtypeStruct(key.shape, jnp.bfloat16),
            jax.ShapeDtypeStruct(key.shape, jnp.bfloat16),
            jax.ShapeDtypeStruct(key.shape, jnp.float32),
        ],
        compiler_params=params(),
        name="finish",
    )(ids, key, value, *pieces)


def exchange(pieces, n):
    return [
        piece if k == 0 else lax.ppermute(piece, "seq", [(i, i ^ k) for i in range(n)])
        for k, piece in enumerate(pieces)
    ]


def fast_shards(grad_out, out_weight, query_gate, key_branch, value_branch, filter_taps):
    n = lax.axis_size("seq")
    planes = lax.axis_size("ch")
    me = lax.axis_index("seq")
    plane = lax.axis_index("ch")
    rows = grad_out.shape[0]
    factor = 1.0 / math.sqrt(rows * n)
    forward, back = half_tables(2 * rows)
    low = plane < planes // 2
    ids = jnp.stack(
        [
            me,
            plane,
            jnp.where((plane == 0) | (plane == planes - 1), 1, 0),
            plane ^ 1,
            jnp.where(low, 2, 1),
            jnp.where(low, 3, 0),
        ]
    ).astype(jnp.int32)

    outer = [(i, i ^ 1) for i in range(planes)]
    inner = [(1, 2), (2, 1), (0, 0), (3, 3)]
    size = rows // CHUNKS
    own = [grad_out[c * size : (c + 1) * size] for c in range(CHUNKS)]
    outer_0 = [lax.ppermute(x, "ch", outer) for x in own]
    inner_0 = [lax.ppermute(x, "ch", inner) for x in own]
    outer_1 = [lax.ppermute(x, "ch", outer) for x in inner_0]
    inner_1 = [lax.ppermute(x, "ch", inner) for x in outer_0]
    outer_2 = [lax.ppermute(x, "ch", outer) for x in inner_1]

    taps_input = exchange(pack(ids, key_branch, value_branch, filter_taps, n), n)
    total = mix(ids, 1, [(grad_out,)], out_weight, None, n)
    kern = tap_kernels(ids, forward, taps_input)
    total = mix(ids, 3, [(x,) for x in outer_0], out_weight, total, n)
    total = mix(ids, 4, list(zip(outer_1, inner_0)), out_weight, total, n)
    gated = [
        exchange(mix_gate(ids, 5, (outer_2[c], inner_1[c]), out_weight, total, query_gate, c, n), n)
        for c in range(CHUNKS)
    ]
    results = exchange(correlate(ids, forward, back, kern, list(zip(*gated))), n)
    return finish(ids, key_branch, value_branch, results, factor)


def solution(mesh):
    specs = dict(
        mesh=mesh,
        in_specs=(
            P("seq", "ch"),
            P("ch", None),
            P("seq", "ch"),
            P("seq", "ch"),
            P("seq", "ch"),
            P("seq", "ch"),
        ),
        out_specs=(P("seq", "ch"), P("seq", "ch"), P("seq", "ch")),
        check_vma=False,
    )
    n, planes = mesh.shape["seq"], mesh.shape["ch"]

    def step(*arrays):
        whole_tiles = arrays[1].shape[0] // planes % (n * LANES) == 0
        fits = whole_tiles and planes == 4 and n & (n - 1) == 0
        return jax.shard_map(fast_shards if fits else shards, **specs)(*arrays)

    return step
```

```python
import functools
import math

import jax
import jax.numpy as jnp
import ml_dtypes
import numpy as np
from jax import lax
from jax.experimental import pallas as pl
from jax.experimental.pallas import tpu as pltpu
from jax.sharding import PartitionSpec as P

LANES = 128
CHUNKS = 2


def build_tables(seg_len):
    twice_length = 2 * seg_len
    freq_index = jnp.arange(twice_length, dtype=jnp.int32)
    row_index = jnp.arange(seg_len, dtype=jnp.int32)
    angle_unit = 2.0 * math.pi / twice_length
    fwd_phase = (freq_index[:, None] * row_index[None, :] % twice_length).astype(
        jnp.float32
    ) * angle_unit
    back_phase = (freq_index[None, :] * (seg_len - row_index[:, None]) % twice_length).astype(
        jnp.float32
    ) * angle_unit
    window_pos = (freq_index + seg_len) % twice_length
    window_phase = (freq_index[None, :] * window_pos[:, None] % twice_length).astype(
        jnp.float32
    ) * angle_unit
    parity = jnp.where(freq_index % 2 == 0, 1.0, -1.0).astype(jnp.float32)[:, None]
    return (
        jnp.cos(fwd_phase).astype(jnp.bfloat16),
        jnp.sin(fwd_phase).astype(jnp.bfloat16),
        jnp.cos(back_phase).astype(jnp.bfloat16),
        jnp.sin(back_phase).astype(jnp.bfloat16),
        jnp.cos(window_phase).astype(jnp.bfloat16),
        jnp.sin(window_phase).astype(jnp.bfloat16),
        parity,
    )


def spectra(block_list, cosine_forward, sine_forward):
    cosine_piece = jnp.einsum(
        "qk,rkb->rqb", cosine_forward, block_list, preferred_element_type=jnp.float32
    )
    sine_piece = jnp.einsum(
        "qk,rkb->rqb", sine_forward, block_list, preferred_element_type=jnp.float32
    )
    return (cosine_piece, sine_piece)


def shards(grad_out, out_weight, query_gate, key_branch, value_branch, filter_taps):
    seg_len = query_gate.shape[0]
    channels = query_gate.shape[1]
    twice_length = 2 * seg_len
    segments = lax.axis_size("seq")
    my_index = lax.axis_index("seq")
    factor = 1.0 / math.sqrt(seg_len * segments)
    grad_mix = lax.dot_general(
        lax.all_gather(grad_out, "ch", axis=1, tiled=True),
        out_weight,
        (((1,), (1,)), ((), ())),
        preferred_element_type=jnp.float32,
    )
    gated_grad = (grad_mix * query_gate.astype(jnp.float32)).astype(jnp.bfloat16)
    conv_input = (key_branch.astype(jnp.float32) * value_branch.astype(jnp.float32)).astype(
        jnp.bfloat16
    )
    tables = build_tables(seg_len)
    (
        cosine_forward,
        sine_forward,
        cosine_backward,
        sine_backward,
        cosine_window,
        sine_window,
        parity,
    ) = tables
    all_taps = lax.all_gather(filter_taps, "seq", axis=0, tiled=True)
    tap_cos, tap_sin = spectra(
        all_taps.reshape(segments, seg_len, channels), cosine_forward, sine_forward
    )
    kern_cos = jnp.concatenate([jnp.zeros_like(tap_cos[:1]), tap_cos[:-1]], 0) + parity * tap_cos
    kern_sin = jnp.concatenate([jnp.zeros_like(tap_sin[:1]), tap_sin[:-1]], 0) + parity * tap_sin
    own_cos, own_sin = spectra(conv_input[None], cosine_forward, sine_forward)
    own_cos = own_cos[0]
    own_sin = own_sin[0]
    zero_spec = jnp.zeros((twice_length, channels), jnp.float32)
    initial = (zero_spec, zero_spec, jnp.zeros(((segments + 1) * seg_len, channels), jnp.float32))
    piece_data = lax.all_gather(gated_grad, "seq", axis=0, tiled=True)
    block_count = piece_data.shape[0] // seg_len
    seg_ids = jnp.arange(block_count, dtype=jnp.int32)
    block_list = piece_data.reshape(block_count, seg_len, channels)
    grad_cos, grad_sin = spectra(block_list, cosine_forward, sine_forward)
    lag_steps = seg_ids - my_index
    inside = seg_ids < segments
    live_mask = ((lag_steps >= 0) & inside).astype(jnp.float32)[:, None, None]
    lag_clip = jnp.clip(lag_steps, 0, segments - 1)
    lag_kcos = jnp.take(kern_cos, lag_clip, axis=0)
    lag_ksin = jnp.take(kern_sin, lag_clip, axis=0)
    running_real = jnp.sum(live_mask * (grad_cos * lag_kcos + grad_sin * lag_ksin), axis=0)
    running_imaginary = jnp.sum(live_mask * (grad_sin * lag_kcos - grad_cos * lag_ksin), axis=0)
    product_real = (own_cos * grad_cos + own_sin * grad_sin).astype(jnp.bfloat16)
    product_imaginary = (own_sin * grad_cos - own_cos * grad_sin).astype(jnp.bfloat16)
    windows = jnp.einsum(
        "an,hny->hay", cosine_window, product_real, preferred_element_type=jnp.float32
    ) - jnp.einsum(
        "an,hny->hay", sine_window, product_imaginary, preferred_element_type=jnp.float32
    )
    windows = windows * (live_mask / twice_length)

    def place(item_index, buffer):
        offset = lag_clip[item_index] * seg_len
        current = lax.dynamic_slice_in_dim(buffer, offset, twice_length, 0)
        return lax.dynamic_update_slice_in_dim(buffer, current + windows[item_index], offset, 0)

    buffer = lax.fori_loop(0, block_list.shape[0], place, initial[2])
    convolution_gradient = (
        jnp.dot(
            cosine_backward, running_real.astype(jnp.bfloat16), preferred_element_type=jnp.float32
        )
        - jnp.dot(
            sine_backward,
            running_imaginary.astype(jnp.bfloat16),
            preferred_element_type=jnp.float32,
        )
    ) / twice_length
    own_rows = lax.psum_scatter(
        buffer[seg_len:].astype(jnp.bfloat16), "seq", scatter_dimension=0, tiled=True
    ).astype(jnp.float32)
    filter_grad = own_rows * factor
    key_grad = (convolution_gradient * value_branch.astype(jnp.float32)).astype(jnp.bfloat16)
    value_grad = (convolution_gradient * key_branch.astype(jnp.float32)).astype(jnp.bfloat16)
    return (key_grad, value_grad, filter_grad)


def half_tables(rows):
    size = 2 * rows
    freq = np.arange(rows)
    pos = np.arange(rows)
    angle = 2.0 * np.pi * (np.outer(freq, pos) % size) / size
    sine = np.sin(angle)
    sine[0] = (-1.0) ** pos
    forward = np.concatenate([np.cos(angle), sine], 0)
    angle = 2.0 * np.pi * (np.outer(rows - pos, freq) % size) / size
    cos_back = 2.0 * np.cos(angle)
    sin_back = -2.0 * np.sin(angle)
    cos_back[:, 0] = 1.0
    sin_back[:, 0] = (-1.0) ** (rows - pos)
    back = np.concatenate([cos_back, sin_back], 1) / size
    return forward.astype(ml_dtypes.bfloat16), back.astype(ml_dtypes.bfloat16)


CHIP, CORE, OUTER, BLOCKS = 0, 1, 2, 3
ANY = pl.BlockSpec(memory_space=pl.ANY)
VMEM = pl.BlockSpec(memory_space=pltpu.VMEM)


def call(kernel, ids, args, in_specs, outs, out_specs, name, scratch=(), flops=0, moved=0, limit=16):
    return pl.pallas_call(
        kernel,
        grid_spec=pltpu.PrefetchScalarGridSpec(
            num_scalar_prefetch=1,
            grid=(1,),
            in_specs=in_specs,
            out_specs=out_specs,
            scratch_shapes=scratch,
        ),
        out_shape=outs,
        compiler_params=pltpu.CompilerParams(vmem_limit_bytes=limit * 2**20),
        cost_estimate=pl.CostEstimate(flops=flops, bytes_accessed=moved, transcendentals=0),
        name=name,
    )(ids, *args)


def whole(x):
    return pl.BlockSpec(x.shape, lambda *_: (0,) * len(x.shape))


def array(shape, dtype=jnp.bfloat16):
    return jax.ShapeDtypeStruct(shape, dtype)


def place(ids, k, core, width):
    return pl.multiple_of(((ids[CHIP] ^ k) * 2 + core) * width, width)


def load_kernel(chips, ids, weight, grad, held, second, sem):
    width = held.shape[1]
    copies = []
    for b in range(4):
        depth = held.shape[2] // 4
        at = pl.multiple_of(ids[BLOCKS + b] * depth, depth)
        for k in range(chips):
            rows = pl.ds(place(ids, k, ids[CORE], width), width)
            copies.append(
                pltpu.make_async_copy(
                    weight.at[rows, pl.ds(at, depth)],
                    held.at[k, :, pl.ds(b * depth, depth)],
                    sem.at[b * chips + k],
                )
            )
    half = second.shape[0]
    copies.append(pltpu.make_async_copy(grad.at[pl.ds(half, half)], second, sem.at[4 * chips]))
    for copy in copies:
        copy.start()
    for copy in copies:
        copy.wait()


def load(ids, weight, grad, chips):
    width = weight.shape[0] // (2 * chips)
    held = (chips, width, weight.shape[1])
    second = (grad.shape[0] // 2, grad.shape[1])
    return call(
        functools.partial(load_kernel, chips),
        ids,
        (weight, grad),
        [ANY, ANY],
        [pltpu.VMEM(held, weight.dtype), array(second)],
        [VMEM, ANY],
        "load_weight",
        [pltpu.SemaphoreType.DMA((4 * chips + 1,))],
        moved=2 * math.prod(held),
    )


def pack_kernel(chips, ids, gate, key, value, taps, out):
    width = out.shape[3]
    for k in range(chips):
        here = (slice(None), pl.ds(place(ids, k, 1 - ids[CORE], width), width))
        out[0, k] = gate[here]
        out[1, k] = taps[here]
        out[2, k] = (key[here].astype(jnp.float32) * value[here].astype(jnp.float32)).astype(jnp.bfloat16)


def pack(ids, gate, key, value, taps, chips):
    rows, channels = key.shape
    out = (3, chips, rows, channels // (2 * chips))
    return call(
        functools.partial(pack_kernel, chips),
        ids,
        (gate, key, value, taps),
        [whole(key)] * 4,
        array(out),
        whole(array(out)),
        "pack_core",
        moved=8 * key.size,
    )


def merge_kernel(chips, ids, gate, key, value, taps, other, gates, *outs):
    width = other.shape[3]
    mine, theirs = ids[CORE], 1 - ids[CORE]
    for k, out in enumerate(outs):
        here = (slice(None), pl.ds(place(ids, k, mine, width), width))
        gates[k, 0] = gate[here]
        gates[k, 1] = other[0, k]
        out[0, mine] = taps[here]
        out[0, theirs] = other[1, k]
        out[1, mine] = (key[here].astype(jnp.float32) * value[here].astype(jnp.float32)).astype(jnp.bfloat16)
        out[1, theirs] = other[2, k]


def merge(ids, gate, key, value, taps, other, chips):
    rows, channels = key.shape
    width = channels // (2 * chips)
    piece = array((2, 2, rows, width))
    gates = array((chips, 2, rows, width))
    out = call(
        functools.partial(merge_kernel, chips),
        ids,
        (gate, key, value, taps, other),
        [whole(key)] * 4 + [whole(other)],
        [gates] + [piece] * chips,
        [whole(gates)] + [whole(piece)] * chips,
        "merge_cores",
        moved=12 * key.size,
    )
    return out[0], out[1:]


def contract(x, w):
    return lax.dot_general(x, w, (((1,), (1,)), ((), ())), preferred_element_type=jnp.float32)


def fetch(ids, groups, x, sem):
    rows = groups[0][0].shape[0]
    for i, group in enumerate(groups):
        to = x.at[pl.ds(i * rows, rows)]
        for j, ref in enumerate(group):
            copy = pltpu.make_async_copy(ref, to, sem.at[i])
            if len(group) == 1:
                copy.start()
            else:
                pl.when(ids[OUTER] == 1 - j)(copy.start)
    for i, group in enumerate(groups):
        pltpu.make_async_copy(group[0], x.at[pl.ds(i * rows, rows)], sem.at[i]).wait()


def grouped(refs, sizes):
    refs = list(refs)
    return [[refs.pop(0) for _ in range(s)] for s in sizes]


def mix_kernel(block, sizes, has_total, ids, *refs):
    count = sum(sizes)
    groups = grouped(refs[:count], sizes)
    held, *rest = refs[count:]
    total, out, x, sem = rest if has_total else (None, *rest)
    depth = x.shape[1]
    fetch(ids, groups, x, sem)

    @pl.loop(0, held.shape[0])
    def _(k):
        value = contract(x[...], held[k, :, block * depth : (block + 1) * depth])
        out[k] = value + total[k] if has_total else value


def mix(ids, block, groups, held, total):
    chips, width, _ = held.shape
    sizes = [len(g) for g in groups]
    flat = [x for g in groups for x in g]
    rows = sum(g[0].shape[0] for g in groups)
    depth = flat[0].shape[1]
    out = (chips, rows, width)
    return call(
        functools.partial(mix_kernel, block, sizes, total is not None),
        ids,
        (*flat, held) + ((total,) if total is not None else ()),
        [ANY] * len(flat) + [VMEM] + ([VMEM] if total is not None else []),
        pltpu.VMEM(out, jnp.float32),
        VMEM,
        "mix",
        [pltpu.VMEM((rows, depth), jnp.bfloat16), pltpu.SemaphoreType.DMA((len(groups),))],
        flops=2 * rows * depth * chips * width,
    )


def gate_kernel(chunk, parts, sizes, ids, *refs):
    count = sum(sizes)
    groups = grouped(refs[:count], sizes)
    held, total, gates, *outs, x, sem = refs[count:]
    depth = x.shape[1]
    rows = x.shape[0] // 2
    own_rows = rows * parts
    fetch(ids, groups, x, sem)
    for k, out in enumerate(outs):
        value = contract(x[...], held[k, :, 3 * depth : 4 * depth])
        for h, core in enumerate((ids[CORE], 1 - ids[CORE])):
            at = 2 * rows * chunk + h * rows
            mixed = total[k, at : at + rows] + value[h * rows : (h + 1) * rows]
            gate = gates[k, h, chunk * rows : (chunk + 1) * rows].astype(jnp.float32)
            out[core] = (mixed * gate).astype(jnp.bfloat16)


def mix_gate(ids, chunk, parts, groups, held, total, gates):
    chips, width, _ = held.shape
    sizes = [len(g) for g in groups]
    flat = [x for g in groups for x in g]
    rows, depth = flat[0].shape
    piece = array((2, rows, width))
    return call(
        functools.partial(gate_kernel, chunk, parts, sizes),
        ids,
        (*flat, held, total, gates),
        [ANY] * len(flat) + [VMEM, VMEM, whole(gates)],
        [piece] * chips,
        [whole(piece)] * chips,
        "mix_gate",
        [pltpu.VMEM((2 * rows, depth), jnp.bfloat16), pltpu.SemaphoreType.DMA((len(groups),))],
        flops=4 * rows * depth * chips * width,
    )


def tap_kernel(ids, forward, *refs):
    *pieces, out, spec = refs
    segs = len(pieces)
    seg = forward.shape[1]
    width = pieces[0].shape[3]
    row = lax.broadcasted_iota(jnp.int32, (2 * seg, width), 0)
    sign = jnp.where(row % 2 == 0, 1.0, -1.0)
    for x in range(2):
        for k, piece in enumerate(pieces):
            block = piece[x].reshape(seg, width)
            spec[ids[CHIP] ^ k] = jnp.dot(forward[...], block, preferred_element_type=jnp.float32)
        for r in range(segs):
            kern = sign * spec[r]
            if r:
                kern += spec[r - 1]
            out[x, r] = kern.astype(jnp.bfloat16)


def tap_kernels(ids, forward, pieces):
    segs = len(pieces)
    width = pieces[0].shape[3]
    shape = (2, segs, *forward.shape[:1], width)
    return call(
        tap_kernel,
        ids,
        (forward, *pieces),
        [whole(forward)] + [whole(p) for p in pieces],
        pltpu.VMEM(shape, jnp.bfloat16),
        VMEM,
        "kernels",
        [pltpu.VMEM(shape[1:], jnp.float32)],
        flops=2 * math.prod(shape) * forward.shape[1],
    )


def correlate_kernel(parts, ids, forward, back, kern, *refs):
    segs = kern.shape[1]
    n = 2 * segs
    pieces = refs[: segs * parts]
    outs = refs[segs * parts : segs * parts + n]
    data, spec, acc, result = refs[segs * parts + n :]
    part = pieces[0].shape[1]
    rows = part * parts
    seg = 2 * rows
    width = data.shape[2]
    for k in range(segs):
        for c in range(parts):
            for core in range(2):
                at = core * rows + c * part
                data[ids[CHIP] ^ k, at : at + part] = pieces[k * parts + c][core]
    for i in range(segs):
        spec[i] = jnp.dot(forward[...], data[i], preferred_element_type=jnp.float32)

    tile = 16

    def products(x, row, lane, first):
        here = (pl.ds(row, tile), pl.ds(lane, LANES))
        there = (pl.ds(row + seg, tile), pl.ds(lane, LANES))
        g_real = [spec[(i, *here)] for i in range(segs)]
        g_imag = [spec[(i, *there)] for i in range(segs)]
        k_real = [kern[(x, r, *here)].astype(jnp.float32) for r in range(segs)]
        k_imag = [kern[(x, r, *there)].astype(jnp.float32) for r in range(segs)]
        if first:
            edge = lax.broadcasted_iota(jnp.int32, (tile, LANES), 0) == 0
        for j in range(segs):
            both = sum(g_real[i] * k_real[i - j] for i in range(j, segs))
            other = sum(g_imag[i] * k_imag[i - j] for i in range(j, segs))
            cross = sum(g_imag[i] * k_real[i - j] - g_real[i] * k_imag[i - j] for i in range(j, segs))
            if first:
                real = both + jnp.where(edge, 0.0, other)
                cross = jnp.where(edge, other, cross)
            else:
                real = both + other
            acc[(j, *here)] = real.astype(jnp.bfloat16)
            acc[(j, *there)] = cross.astype(jnp.bfloat16)

    for x in range(2):
        for lane in range(0, width, LANES):
            products(x, 0, lane, True)

            @pl.loop(1, seg // tile)
            def _(t):
                products(x, pl.multiple_of(t * tile, tile), lane, False)

        for j in range(segs):
            value = jnp.dot(back[...], acc[j], preferred_element_type=jnp.float32).astype(jnp.bfloat16)
            for core in range(2):
                result[2 * j + core, x] = value[core * rows : (core + 1) * rows]
    me = 2 * ids[CHIP] + ids[CORE]
    for k in range(n):
        outs[k][...] = result[me ^ k]


def correlate(ids, forward, back, kern, pieces):
    segs, parts = len(pieces), len(pieces[0])
    flat = [p for group in pieces for p in group]
    width = flat[0].shape[2]
    rows = flat[0].shape[1] * parts
    seg = 2 * rows
    n = 2 * segs
    out = array((2, rows, width))
    return call(
        functools.partial(correlate_kernel, parts),
        ids,
        (forward, back, kern, *flat),
        [whole(forward), whole(back), VMEM] + [whole(p) for p in flat],
        [out] * n,
        [whole(out)] * n,
        "correlate",
        [
            pltpu.VMEM((segs, seg, width), jnp.bfloat16),
            pltpu.VMEM((segs, 2 * seg, width), jnp.float32),
            pltpu.VMEM((segs, 2 * seg, width), jnp.bfloat16),
            pltpu.VMEM((n, *out.shape), jnp.bfloat16),
        ],
        flops=2 * segs * seg * seg * 2 * width * 3,
    )


def finish_kernel(factor, ids, key, value, *refs):
    n = len(refs) - 11
    pieces = refs[:n]
    outs = refs[n : n + 3]
    key_v, value_v, piece_v, key_o, value_o, filter_o, in_sem, out_sem = refs[n + 3 :]
    width = piece_v.shape[3]
    me = 2 * ids[CHIP] + ids[CORE]
    loads = [pltpu.make_async_copy(p, piece_v.at[k], in_sem.at[k]) for k, p in enumerate(pieces)]
    loads += [pltpu.make_async_copy(key, key_v, in_sem.at[n]), pltpu.make_async_copy(value, value_v, in_sem.at[n + 1])]
    for copy in loads[::-1]:
        copy.start()
    for copy in loads[n:]:
        copy.wait()
    stores = []
    for k in range(n):
        here = (slice(None), pl.ds(pl.multiple_of((me ^ k) * width, width), width))
        loads[k].wait()
        conv_grad = piece_v[k, 0].astype(jnp.float32)
        key_o[here] = (conv_grad * value_v[here].astype(jnp.float32)).astype(jnp.bfloat16)
        value_o[here] = (conv_grad * key_v[here].astype(jnp.float32)).astype(jnp.bfloat16)
        filter_o[here] = piece_v[k, 1].astype(jnp.float32) * factor
        for o, (src, dst) in enumerate(zip((key_o, value_o, filter_o), outs)):
            stores.append(pltpu.make_async_copy(src.at[here], dst.at[here], out_sem.at[o, k]))
            stores[-1].start()
    for copy in stores:
        copy.wait()


def finish(ids, key, value, pieces, factor):
    n = len(pieces)
    outs = [array(key.shape), array(key.shape), array(key.shape, jnp.float32)]
    return call(
        functools.partial(finish_kernel, factor),
        ids,
        (key, value, *pieces),
        [ANY] * (2 + n),
        outs,
        [ANY] * 3,
        "finish",
        [
            pltpu.VMEM(key.shape, key.dtype),
            pltpu.VMEM(key.shape, key.dtype),
            pltpu.VMEM((n, *pieces[0].shape), pieces[0].dtype),
            *[pltpu.VMEM(o.shape, o.dtype) for o in outs],
            pltpu.SemaphoreType.DMA((n + 2,)),
            pltpu.SemaphoreType.DMA((3, n)),
        ],
        moved=12 * key.size,
    )


def swap(x, k, n):
    return lax.ppermute(x, "seq", [(i, i ^ k) for i in range(n)]) if k else x


def fast_shards(grad_out, out_weight, query_gate, key_branch, value_branch, filter_taps):
    n = lax.axis_size("seq")
    planes = lax.axis_size("ch")
    me = lax.axis_index("seq")
    plane = lax.axis_index("ch")
    rows = grad_out.shape[0]
    chips = n // 2
    factor = 1.0 / math.sqrt(rows * n)
    forward, back = half_tables(2 * rows)
    low = plane < planes // 2
    ids = jnp.stack(
        [
            me // 2,
            me % 2,
            jnp.where((plane == 0) | (plane == planes - 1), 1, 0),
            plane,
            plane ^ 1,
            jnp.where(low, 2, 1),
            jnp.where(low, 3, 0),
        ]
    ).astype(jnp.int32)

    outer = [(i, i ^ 1) for i in range(planes)]
    inner = []
    for s in range(n):
        inner += [(s * planes + 1, s * planes + 2), (s * planes + 2, s * planes + 1)]
        inner += [(s * planes + z, (s ^ 1) * planes + z) for z in (0, planes - 1)]

    def send_outer(x):
        return lax.ppermute(x, "ch", outer)

    def send_inner(x):
        return lax.ppermute(x, ("seq", "ch"), inner)

    def both(*candidates):
        return [list(candidates), [swap(x, 1, n) for x in candidates]]

    held, second = load(ids, out_weight, grad_out, chips)
    own = [grad_out[: rows // CHUNKS], second]
    outer_0 = [send_outer(x) for x in own]
    inner_0 = [send_inner(x) for x in own]
    outer_1 = [send_outer(x) for x in inner_0]
    inner_1 = [send_inner(x) for x in outer_0]
    outer_2 = [send_outer(x) for x in inner_1]

    other = swap(pack(ids, query_gate, key_branch, value_branch, filter_taps, chips), 1, n)
    gates, taps_input = merge(ids, query_gate, key_branch, value_branch, filter_taps, other, chips)
    taps_input = [swap(x, 2 * k, n) for k, x in enumerate(taps_input)]

    total = mix(ids, 0, [g for x in own for g in both(x)], held, None)
    total = mix(ids, 1, [g for x in outer_0 for g in both(x)], held, total)
    total = mix(ids, 2, [g for x in zip(outer_1, inner_0) for g in both(*x)], held, total)
    kern = tap_kernels(ids, forward, taps_input)
    gated = []
    for c, x in enumerate(zip(outer_2, inner_1)):
        pieces = mix_gate(ids, c, CHUNKS, both(*x), held, total, gates)
        gated.append([swap(p, 2 * k, n) for k, p in enumerate(pieces)])
    results = correlate(ids, forward, back, kern, list(zip(*gated)))
    results = [swap(x, k, n) for k, x in enumerate(results)]
    return finish(ids, key_branch, value_branch, results, factor)


def solution(mesh):
    specs = dict(
        mesh=mesh,
        in_specs=(
            P("seq", "ch"),
            P("ch", None),
            P("seq", "ch"),
            P("seq", "ch"),
            P("seq", "ch"),
            P("seq", "ch"),
        ),
        out_specs=(P("seq", "ch"), P("seq", "ch"), P("seq", "ch")),
        check_vma=False,
    )
    n, planes = mesh.shape["seq"], mesh.shape["ch"]

    def step(*arrays):
        whole_tiles = arrays[1].shape[0] // planes % (n * LANES) == 0
        fits = whole_tiles and planes == 4 and n & (n - 1) == 0
        return jax.shard_map(fast_shards if fits else shards, **specs)(*arrays)

    return step
```

```python
import functools
import math

import jax
import jax.numpy as jnp
import ml_dtypes
import numpy as np
from jax import lax
from jax.experimental import pallas as pl
from jax.experimental.pallas import tpu as pltpu
from jax.sharding import PartitionSpec as P

LANES = 128
CHUNKS = 2


def build_tables(seg_len):
    twice_length = 2 * seg_len
    freq_index = jnp.arange(twice_length, dtype=jnp.int32)
    row_index = jnp.arange(seg_len, dtype=jnp.int32)
    angle_unit = 2.0 * math.pi / twice_length
    fwd_phase = (freq_index[:, None] * row_index[None, :] % twice_length).astype(
        jnp.float32
    ) * angle_unit
    back_phase = (freq_index[None, :] * (seg_len - row_index[:, None]) % twice_length).astype(
        jnp.float32
    ) * angle_unit
    window_pos = (freq_index + seg_len) % twice_length
    window_phase = (freq_index[None, :] * window_pos[:, None] % twice_length).astype(
        jnp.float32
    ) * angle_unit
    parity = jnp.where(freq_index % 2 == 0, 1.0, -1.0).astype(jnp.float32)[:, None]
    return (
        jnp.cos(fwd_phase).astype(jnp.bfloat16),
        jnp.sin(fwd_phase).astype(jnp.bfloat16),
        jnp.cos(back_phase).astype(jnp.bfloat16),
        jnp.sin(back_phase).astype(jnp.bfloat16),
        jnp.cos(window_phase).astype(jnp.bfloat16),
        jnp.sin(window_phase).astype(jnp.bfloat16),
        parity,
    )


def spectra(block_list, cosine_forward, sine_forward):
    cosine_piece = jnp.einsum(
        "qk,rkb->rqb", cosine_forward, block_list, preferred_element_type=jnp.float32
    )
    sine_piece = jnp.einsum(
        "qk,rkb->rqb", sine_forward, block_list, preferred_element_type=jnp.float32
    )
    return (cosine_piece, sine_piece)


def shards(grad_out, out_weight, query_gate, key_branch, value_branch, filter_taps):
    seg_len = query_gate.shape[0]
    channels = query_gate.shape[1]
    twice_length = 2 * seg_len
    segments = lax.axis_size("seq")
    my_index = lax.axis_index("seq")
    factor = 1.0 / math.sqrt(seg_len * segments)
    grad_mix = lax.dot_general(
        lax.all_gather(grad_out, "ch", axis=1, tiled=True),
        out_weight,
        (((1,), (1,)), ((), ())),
        preferred_element_type=jnp.float32,
    )
    gated_grad = (grad_mix * query_gate.astype(jnp.float32)).astype(jnp.bfloat16)
    conv_input = (key_branch.astype(jnp.float32) * value_branch.astype(jnp.float32)).astype(
        jnp.bfloat16
    )
    tables = build_tables(seg_len)
    (
        cosine_forward,
        sine_forward,
        cosine_backward,
        sine_backward,
        cosine_window,
        sine_window,
        parity,
    ) = tables
    all_taps = lax.all_gather(filter_taps, "seq", axis=0, tiled=True)
    tap_cos, tap_sin = spectra(
        all_taps.reshape(segments, seg_len, channels), cosine_forward, sine_forward
    )
    kern_cos = jnp.concatenate([jnp.zeros_like(tap_cos[:1]), tap_cos[:-1]], 0) + parity * tap_cos
    kern_sin = jnp.concatenate([jnp.zeros_like(tap_sin[:1]), tap_sin[:-1]], 0) + parity * tap_sin
    own_cos, own_sin = spectra(conv_input[None], cosine_forward, sine_forward)
    own_cos = own_cos[0]
    own_sin = own_sin[0]
    zero_spec = jnp.zeros((twice_length, channels), jnp.float32)
    initial = (zero_spec, zero_spec, jnp.zeros(((segments + 1) * seg_len, channels), jnp.float32))
    piece_data = lax.all_gather(gated_grad, "seq", axis=0, tiled=True)
    block_count = piece_data.shape[0] // seg_len
    seg_ids = jnp.arange(block_count, dtype=jnp.int32)
    block_list = piece_data.reshape(block_count, seg_len, channels)
    grad_cos, grad_sin = spectra(block_list, cosine_forward, sine_forward)
    lag_steps = seg_ids - my_index
    inside = seg_ids < segments
    live_mask = ((lag_steps >= 0) & inside).astype(jnp.float32)[:, None, None]
    lag_clip = jnp.clip(lag_steps, 0, segments - 1)
    lag_kcos = jnp.take(kern_cos, lag_clip, axis=0)
    lag_ksin = jnp.take(kern_sin, lag_clip, axis=0)
    running_real = jnp.sum(live_mask * (grad_cos * lag_kcos + grad_sin * lag_ksin), axis=0)
    running_imaginary = jnp.sum(live_mask * (grad_sin * lag_kcos - grad_cos * lag_ksin), axis=0)
    product_real = (own_cos * grad_cos + own_sin * grad_sin).astype(jnp.bfloat16)
    product_imaginary = (own_sin * grad_cos - own_cos * grad_sin).astype(jnp.bfloat16)
    windows = jnp.einsum(
        "an,hny->hay", cosine_window, product_real, preferred_element_type=jnp.float32
    ) - jnp.einsum(
        "an,hny->hay", sine_window, product_imaginary, preferred_element_type=jnp.float32
    )
    windows = windows * (live_mask / twice_length)

    def place(item_index, buffer):
        offset = lag_clip[item_index] * seg_len
        current = lax.dynamic_slice_in_dim(buffer, offset, twice_length, 0)
        return lax.dynamic_update_slice_in_dim(buffer, current + windows[item_index], offset, 0)

    buffer = lax.fori_loop(0, block_list.shape[0], place, initial[2])
    convolution_gradient = (
        jnp.dot(
            cosine_backward, running_real.astype(jnp.bfloat16), preferred_element_type=jnp.float32
        )
        - jnp.dot(
            sine_backward,
            running_imaginary.astype(jnp.bfloat16),
            preferred_element_type=jnp.float32,
        )
    ) / twice_length
    own_rows = lax.psum_scatter(
        buffer[seg_len:].astype(jnp.bfloat16), "seq", scatter_dimension=0, tiled=True
    ).astype(jnp.float32)
    filter_grad = own_rows * factor
    key_grad = (convolution_gradient * value_branch.astype(jnp.float32)).astype(jnp.bfloat16)
    value_grad = (convolution_gradient * key_branch.astype(jnp.float32)).astype(jnp.bfloat16)
    return (key_grad, value_grad, filter_grad)


def half_tables(rows):
    size = 2 * rows
    freq = np.arange(rows)
    pos = np.arange(rows)
    angle = 2.0 * np.pi * (np.outer(freq, pos) % size) / size
    sine = np.sin(angle)
    sine[0] = (-1.0) ** pos
    forward = np.concatenate([np.cos(angle), sine], 0)
    angle = 2.0 * np.pi * (np.outer(rows - pos, freq) % size) / size
    cos_back = 2.0 * np.cos(angle)
    sin_back = -2.0 * np.sin(angle)
    cos_back[:, 0] = 1.0
    sin_back[:, 0] = (-1.0) ** (rows - pos)
    back = np.concatenate([cos_back, sin_back], 1) / size
    return forward.astype(ml_dtypes.bfloat16), back.astype(ml_dtypes.bfloat16)


ANY = pl.BlockSpec(memory_space=pl.ANY)
VMEM = pl.BlockSpec(memory_space=pltpu.VMEM)
MARK = jax.ShapeDtypeStruct((8, LANES), jnp.float32)


class Spot:
    def __init__(self):
        me, plane, planes = lax.axis_index("seq"), lax.axis_index("ch"), lax.axis_size("ch")
        low = plane < planes // 2
        self.chip, self.core = me // 2, me % 2
        self.outer = (plane == 0) | (plane == planes - 1)
        self.blocks = (plane, plane ^ 1, jnp.where(low, 2, 1), jnp.where(low, 3, 0))


def call(kernel, args, in_specs, outs, out_specs, name, scratch=(), limit=24, flops=0, update=(), carry=(), after=()):
    same = (*update, *carry)
    count, results, written = len(args), len(outs), len(outs) + len(update)

    def body(*refs):
        rest = refs[count + len(same) + len(after) :]
        mark, *scratch_refs = rest[results + len(same) :]
        mark[...] = jnp.zeros_like(mark)
        kernel(Spot(), *refs[:count], *rest[:written], *scratch_refs)

    return pl.pallas_call(
        body,
        input_output_aliases={count + i: results + i for i in range(len(same))},
        grid=(1,),
        in_specs=[*in_specs, *[ANY] * (len(same) + len(after))],
        out_specs=[*out_specs, *[ANY] * len(same), whole(MARK)],
        scratch_shapes=scratch,
        out_shape=[*outs, *[array(x.shape, x.dtype) for x in same], MARK],
        compiler_params=pltpu.CompilerParams(vmem_limit_bytes=limit * 2**20),
        cost_estimate=pl.CostEstimate(flops=flops, bytes_accessed=0, transcendentals=0),
        name=name,
    )(*args, *same, *after)


def whole(x):
    return pl.BlockSpec(x.shape, lambda *_: (0,) * len(x.shape))


def array(shape, dtype=jnp.bfloat16):
    return jax.ShapeDtypeStruct(shape, dtype)


def place(spot, k, core, width):
    return pl.multiple_of(((spot.chip ^ k) * 2 + core) * width, width)


def load_kernel(chips, spot, weight, held, sem):
    width = held.shape[1]
    depth = held.shape[2] // 4
    copies = []
    for b in range(4):
        at = pl.multiple_of(spot.blocks[b] * depth, depth)
        for k in range(chips):
            rows = pl.ds(place(spot, k, spot.core, width), width)
            copies.append(
                pltpu.make_async_copy(
                    weight.at[rows, pl.ds(at, depth)],
                    held.at[k, :, pl.ds(b * depth, depth)],
                    sem.at[b * chips + k],
                )
            )
    for copy in copies:
        copy.start()
    for copy in copies:
        copy.wait()


def load(weight, chips, **order):
    held = (chips, weight.shape[0] // (2 * chips), weight.shape[1])
    return call(
        functools.partial(load_kernel, chips),
        (weight,),
        [ANY],
        [pltpu.VMEM(held, weight.dtype)],
        [VMEM],
        "load_weight",
        [pltpu.SemaphoreType.DMA((4 * chips,))],
        **order,
    )


def pack_kernel(chips, spot, gate, key, value, taps, mine, theirs_0, theirs_1, all_in, sem):
    width = mine.shape[3]
    half = theirs_0.shape[2]
    loads = [pltpu.make_async_copy(ref, all_in.at[i], sem.at[i]) for i, ref in enumerate((gate, taps, key, value))]
    for copy in loads:
        copy.start()
    for copy in loads:
        copy.wait()
    upper, lower = slice(0, half), slice(half, 2 * half)
    for out, core, rows in (
        (theirs_0, 1 - spot.core, upper),
        (theirs_1, 1 - spot.core, lower),
        (mine, spot.core, slice(None)),
    ):
        for k in range(chips):
            here = (rows, pl.ds(place(spot, k, core, width), width))
            out[0, k] = all_in[(0, *here)]
            out[1, k] = all_in[(1, *here)]
            product = all_in[(2, *here)].astype(jnp.float32) * all_in[(3, *here)].astype(jnp.float32)
            out[2, k] = product.astype(jnp.bfloat16)


def pack(gate, key, value, taps, chips, **order):
    rows, channels = key.shape
    out = (3, chips, rows, channels // (2 * chips))
    half = array((3, chips, rows // 2, channels // (2 * chips)))
    return call(
        functools.partial(pack_kernel, chips),
        (gate, key, value, taps),
        [ANY] * 4,
        [pltpu.VMEM(out, jnp.bfloat16), half, half],
        [VMEM, whole(half), whole(half)],
        "pack_core",
        [pltpu.VMEM((4, rows, channels), jnp.bfloat16), pltpu.SemaphoreType.DMA((4,))],
        limit=58,
        **order,
    )


def merge_kernel(spot, mine, other_0, other_1, gates, *refs):
    *outs, sem = refs
    own, theirs = spot.core, 1 - spot.core
    half = other_0.shape[2]
    loads = []
    for h, other in enumerate((other_0, other_1)):
        rows = pl.ds(h * half, half)
        for k, out in enumerate(outs):
            for i, to in enumerate((gates.at[k, 1, rows], out.at[0, theirs, rows], out.at[1, theirs, rows])):
                loads.append(pltpu.make_async_copy(other.at[i, k], to, sem.at[len(loads)]))
    for copy in loads:
        copy.start()
    for k, out in enumerate(outs):
        gates[k, 0] = mine[0, k]
        out[0, own] = mine[1, k]
        out[1, own] = mine[2, k]
    for copy in loads:
        copy.wait()


def merge(mine, others, **order):
    _, chips, rows, width = mine.shape
    piece = array((2, 2, rows, width))
    out = call(
        merge_kernel,
        (mine, *others),
        [VMEM, ANY, ANY],
        [pltpu.VMEM((chips, 2, rows, width), jnp.bfloat16)] + [piece] * chips,
        [VMEM] + [whole(piece)] * chips,
        "merge_cores",
        [pltpu.SemaphoreType.DMA((6 * chips,))],
        **order,
    )
    return out[0], out[1 : 1 + chips], out[1 + chips :]


def contract(x, w):
    return lax.dot_general(x, w, (((1,), (1,)), ((), ())), preferred_element_type=jnp.float32)


def fetch(spot, groups, x, sem):
    rows = groups[0][0].shape[0]
    for i, group in enumerate(groups):
        to = x.at[pl.ds(i * rows, rows)]
        for j, ref in enumerate(group):
            copy = pltpu.make_async_copy(ref, to, sem.at[i])
            if len(group) == 1:
                copy.start()
            else:
                pl.when(spot.outer if j == 0 else ~spot.outer)(copy.start)
    for i, group in enumerate(groups):
        pltpu.make_async_copy(group[0], x.at[pl.ds(i * rows, rows)], sem.at[i]).wait()


def grouped(refs, sizes):
    refs = list(refs)
    return [[refs.pop(0) for _ in range(s)] for s in sizes]


def mix_kernel(block, sizes, has_total, spot, *refs):
    count = sum(sizes)
    groups = grouped(refs[:count], sizes)
    held, *rest = refs[count:]
    total, out, x, sem = rest if has_total else (None, *rest)
    depth = x.shape[1]
    fetch(spot, groups, x, sem)

    @pl.loop(0, held.shape[0])
    def _(k):
        value = contract(x[...], held[k, :, block * depth : (block + 1) * depth])
        out[k] = value + total[k] if has_total else value


def mix(block, groups, held, total, **order):
    chips, width, _ = held.shape
    sizes = [len(g) for g in groups]
    flat = [x for g in groups for x in g]
    rows = sum(g[0].shape[0] for g in groups)
    depth = flat[0].shape[1]
    out = (chips, rows, width)
    return call(
        functools.partial(mix_kernel, block, sizes, total is not None),
        (*flat, held) + ((total,) if total is not None else ()),
        [ANY] * len(flat) + [VMEM] + ([VMEM] if total is not None else []),
        [pltpu.VMEM(out, jnp.float32)],
        [VMEM],
        "mix",
        [pltpu.VMEM((rows, depth), jnp.bfloat16), pltpu.SemaphoreType.DMA((len(groups),))],
        **order,
    )


def gate_kernel(chunk, parts, sizes, spot, *refs):
    count = sum(sizes)
    groups = grouped(refs[:count], sizes)
    held, total, gates, *outs, x, sem = refs[count:]
    depth = x.shape[1]
    rows = x.shape[0] // 2
    own_rows = rows * parts
    fetch(spot, groups, x, sem)
    for k, out in enumerate(outs):
        value = contract(x[...], held[k, :, 3 * depth : 4 * depth])
        for h, core in enumerate((spot.core, 1 - spot.core)):
            at = h * own_rows + chunk * rows
            mixed = total[k, at : at + rows] + value[h * rows : (h + 1) * rows]
            gate = gates[k, h, chunk * rows : (chunk + 1) * rows].astype(jnp.float32)
            out[core] = (mixed * gate).astype(jnp.bfloat16)


def mix_gate(chunk, parts, groups, held, total, gates):
    chips, width, _ = held.shape
    sizes = [len(g) for g in groups]
    flat = [x for g in groups for x in g]
    rows, depth = flat[0].shape
    piece = array((2, rows, width))
    return call(
        functools.partial(gate_kernel, chunk, parts, sizes),
        (*flat, held, total, gates),
        [ANY] * len(flat) + [VMEM] * 3,
        [piece] * chips,
        [whole(piece)] * chips,
        "mix_gate",
        [pltpu.VMEM((2 * rows, depth), jnp.bfloat16), pltpu.SemaphoreType.DMA((len(groups),))],
    )


def tap_kernel(spot, forward, *refs):
    *pieces, out, spec = refs
    segs = len(pieces)
    seg = forward.shape[1]
    width = pieces[0].shape[3]
    row = lax.broadcasted_iota(jnp.int32, (2 * seg, width), 0)
    sign = jnp.where(row % 2 == 0, 1.0, -1.0)
    for x in range(2):
        for k, piece in enumerate(pieces):
            block = piece[x].reshape(seg, width)
            spec[spot.chip ^ k] = jnp.dot(forward[...], block, preferred_element_type=jnp.float32)
        for r in range(segs):
            kern = sign * spec[r]
            if r:
                kern += spec[r - 1]
            out[x, r] = kern.astype(jnp.bfloat16)


def tap_kernels(forward, pieces, **order):
    segs = len(pieces)
    width = pieces[0].shape[3]
    shape = (2, segs, *forward.shape[:1], width)
    return call(
        tap_kernel,
        (forward, *pieces),
        [whole(forward)] + [whole(p) for p in pieces],
        [pltpu.VMEM(shape, jnp.bfloat16)],
        [VMEM],
        "kernels",
        [pltpu.VMEM(shape[1:], jnp.float32)],
        flops=12 * math.prod(shape) * forward.shape[1],
        **order,
    )


def correlate_kernel(parts, spot, forward, back, kern, *refs):
    segs = kern.shape[1]
    n = 2 * segs
    pieces = refs[: segs * parts]
    outs = refs[segs * parts : segs * parts + n]
    data, spec, acc, result = refs[segs * parts + n :]
    part = pieces[0].shape[1]
    rows = part * parts
    seg = 2 * rows
    width = data.shape[2]
    for k in range(segs):
        for c in range(parts):
            for core in range(2):
                at = core * rows + c * part
                data[spot.chip ^ k, at : at + part] = pieces[k * parts + c][core]
    for i in range(segs):
        spec[i] = jnp.dot(forward[...], data[i], preferred_element_type=jnp.float32)

    tile = 16

    def products(x, row, lane, first):
        here = (pl.ds(row, tile), pl.ds(lane, LANES))
        there = (pl.ds(row + seg, tile), pl.ds(lane, LANES))
        g_real = [spec[(i, *here)] for i in range(segs)]
        g_imag = [spec[(i, *there)] for i in range(segs)]
        k_real = [kern[(x, r, *here)].astype(jnp.float32) for r in range(segs)]
        k_imag = [kern[(x, r, *there)].astype(jnp.float32) for r in range(segs)]
        if first:
            edge = lax.broadcasted_iota(jnp.int32, (tile, LANES), 0) == 0
        for j in range(segs):
            both = sum(g_real[i] * k_real[i - j] for i in range(j, segs))
            other = sum(g_imag[i] * k_imag[i - j] for i in range(j, segs))
            cross = sum(g_imag[i] * k_real[i - j] - g_real[i] * k_imag[i - j] for i in range(j, segs))
            if first:
                real = both + jnp.where(edge, 0.0, other)
                cross = jnp.where(edge, other, cross)
            else:
                real = both + other
            acc[(j, *here)] = real.astype(jnp.bfloat16)
            acc[(j, *there)] = cross.astype(jnp.bfloat16)

    for x in range(2):
        for lane in range(0, width, LANES):
            products(x, 0, lane, True)

            @pl.loop(1, seg // tile)
            def _(t):
                products(x, pl.multiple_of(t * tile, tile), lane, False)

        for j in range(segs):
            value = jnp.dot(back[...], acc[j], preferred_element_type=jnp.float32).astype(jnp.bfloat16)
            for core in range(2):
                result[2 * j + core, x] = value[core * rows : (core + 1) * rows]
    me = 2 * spot.chip + spot.core
    for k in range(n):
        outs[k][...] = result[me ^ k]


def correlate(forward, back, kern, pieces):
    segs, parts = len(pieces), len(pieces[0])
    flat = [p for group in pieces for p in group]
    width = flat[0].shape[2]
    rows = flat[0].shape[1] * parts
    seg = 2 * rows
    n = 2 * segs
    out = array((2, rows, width))
    return call(
        functools.partial(correlate_kernel, parts),
        (forward, back, kern, *flat),
        [whole(forward), whole(back), VMEM] + [whole(p) for p in flat],
        [out] * n,
        [whole(out)] * n,
        "correlate",
        [
            pltpu.VMEM((segs, seg, width), jnp.bfloat16),
            pltpu.VMEM((segs, 2 * seg, width), jnp.float32),
            pltpu.VMEM((segs, 2 * seg, width), jnp.bfloat16),
            pltpu.VMEM((n, *out.shape), jnp.bfloat16),
        ],
    )


def finish_kernel(ks, factor, fetch_branches, spot, *refs):
    n = len(ks)
    if fetch_branches:
        (key, value, *pieces), refs = refs[: 2 + n], refs[2 + n :]
        branches, *outs, piece_v, key_o, value_o, filter_o, in_sem, out_sem = refs
    else:
        (branches, *pieces), refs = refs[: 1 + n], refs[1 + n :]
        *outs, piece_v, key_o, value_o, filter_o, in_sem, out_sem = refs
    width = piece_v.shape[3]
    me = 2 * spot.chip + spot.core
    loads = [pltpu.make_async_copy(p, piece_v.at[i], in_sem.at[i]) for i, p in enumerate(pieces)]
    if fetch_branches:
        loads.append(pltpu.make_async_copy(key, branches.at[0], in_sem.at[n]))
        loads.append(pltpu.make_async_copy(value, branches.at[1], in_sem.at[n + 1]))
    for copy in loads:
        copy.start()
    for copy in loads:
        copy.wait()
    stores = []
    for i, k in enumerate(ks):
        here = (slice(None), pl.ds(pl.multiple_of((me ^ k) * width, width), width))
        conv_grad = piece_v[i, 0].astype(jnp.float32)
        key_o[i] = (conv_grad * branches[(1, *here)].astype(jnp.float32)).astype(jnp.bfloat16)
        value_o[i] = (conv_grad * branches[(0, *here)].astype(jnp.float32)).astype(jnp.bfloat16)
        filter_o[i] = piece_v[i, 1].astype(jnp.float32) * factor
        for o, (src, dst) in enumerate(zip((key_o, value_o, filter_o), outs)):
            stores.append(pltpu.make_async_copy(src.at[i], dst.at[here], out_sem.at[o, i]))
            stores[-1].start()
    for copy in stores:
        copy.wait()


def finish(ks, pieces, factor, key=None, value=None, branches=None, grads=None):
    begin = branches is None
    n = len(ks)
    rows, width = pieces[0].shape[1:]
    scratch = [
        pltpu.VMEM((n, 2, rows, width), jnp.bfloat16),
        pltpu.VMEM((n, rows, width), jnp.bfloat16),
        pltpu.VMEM((n, rows, width), jnp.bfloat16),
        pltpu.VMEM((n, rows, width), jnp.float32),
        pltpu.SemaphoreType.DMA((n + 2,)),
        pltpu.SemaphoreType.DMA((3, n)),
    ]
    kernel = functools.partial(finish_kernel, ks, factor, begin)
    if begin:
        both = pltpu.VMEM((2, *key.shape), key.dtype)
        outs = [both, array(key.shape), array(key.shape), array(key.shape, jnp.float32)]
        args = (key, value, *pieces)
        return call(kernel, args, [ANY] * len(args), outs, [VMEM, *[ANY] * 3], "finish", scratch)
    args = (branches, *pieces)
    return call(kernel, args, [VMEM, *[ANY] * n], [], [], "finish", scratch, update=grads)


def hold(arrays, after):
    return call(lambda spot: None, (), [], [], [], "hold", carry=arrays, after=after)


def swap(x, k, n):
    return lax.ppermute(x, "seq", [(i, i ^ k) for i in range(n)]) if k else x


def fast_shards(grad_out, out_weight, query_gate, key_branch, value_branch, filter_taps):
    n = lax.axis_size("seq")
    planes = lax.axis_size("ch")
    rows = grad_out.shape[0]
    chips = n // 2
    factor = 1.0 / math.sqrt(rows * n)
    forward, back = (jnp.asarray(t) for t in half_tables(2 * rows))
    outer = [(i, i ^ 1) for i in range(planes)]
    inner = []
    for s in range(n):
        inner += [(s * planes + 1, s * planes + 2), (s * planes + 2, s * planes + 1)]
        inner += [(s * planes + z, (s ^ 1) * planes + z) for z in (0, planes - 1)]

    def send_outer(x):
        return lax.ppermute(x, "ch", outer)

    def send_inner(x):
        return lax.ppermute(x, ("seq", "ch"), inner)

    def other(x):
        return swap(x, 1, n)

    outer_0, inner_0, others = send_outer(grad_out), send_inner(grad_out), other(grad_out)
    mine, *packed, packed_mark = pack(query_gate, key_branch, value_branch, filter_taps, chips)
    gates, taps_input, (merged,) = merge(mine, [other(x) for x in packed], after=[packed_mark])
    taps_input = [swap(x, 2 * k, n) for k, x in enumerate(taps_input)]
    outer_1, inner_1 = send_outer(inner_0), send_inner(outer_0)
    kern, tapped = tap_kernels(forward, taps_input, after=[merged])
    outer_1, inner_1, gone = hold([outer_1, inner_1], after=[tapped])
    outer_2 = send_outer(inner_1)

    held, loaded = load(out_weight, chips, after=[gone])
    total, first = mix(0, [[grad_out], [others]], held, None, after=[loaded])
    total, outer_1, second = mix(1, [[outer_0], [other(outer_0)]], held, total, carry=[outer_1], after=[first])
    blocks = [[outer_1, inner_0], [other(outer_1), other(inner_0)]]
    total, _ = mix(2, blocks, held, total, after=[second])
    gated = mix_gate(0, 1, [[outer_2, inner_1], [other(outer_2), other(inner_1)]], held, total, gates)[:chips]
    gated = [[swap(p, 2 * k, n)] for k, p in enumerate(gated)]

    results = correlate(forward, back, kern, gated)[:n]
    results = [swap(x, k, n) for k, x in enumerate(results)]
    near, far = list(range(n // 2)), list(range(n // 2, n))
    branches, *grads, _ = finish(near, results[: n // 2], factor, key=key_branch, value=value_branch)
    return tuple(finish(far, results[n // 2 :], factor, branches=branches, grads=grads)[:3])


def solution(mesh):
    specs = dict(
        mesh=mesh,
        in_specs=(
            P("seq", "ch"),
            P("ch", None),
            P("seq", "ch"),
            P("seq", "ch"),
            P("seq", "ch"),
            P("seq", "ch"),
        ),
        out_specs=(P("seq", "ch"), P("seq", "ch"), P("seq", "ch")),
        check_vma=False,
    )
    n, planes = mesh.shape["seq"], mesh.shape["ch"]

    def step(*arrays):
        whole_tiles = arrays[1].shape[0] // planes % (n * LANES) == 0
        fits = whole_tiles and planes == 4 and n & (n - 1) == 0
        return jax.shard_map(fast_shards if fits else shards, **specs)(*arrays)

    return step
```

```python
import functools
import math

import jax
import jax.numpy as jnp
import ml_dtypes
import numpy as np
from jax import lax
from jax.experimental import pallas as pl
from jax.experimental.pallas import tpu as pltpu
from jax.sharding import PartitionSpec as P

LANES = 128


def build_tables(seg_len):
    twice_length = 2 * seg_len
    freq_index = jnp.arange(twice_length, dtype=jnp.int32)
    row_index = jnp.arange(seg_len, dtype=jnp.int32)
    angle_unit = 2.0 * math.pi / twice_length
    fwd_phase = (freq_index[:, None] * row_index[None, :] % twice_length).astype(
        jnp.float32
    ) * angle_unit
    back_phase = (freq_index[None, :] * (seg_len - row_index[:, None]) % twice_length).astype(
        jnp.float32
    ) * angle_unit
    window_pos = (freq_index + seg_len) % twice_length
    window_phase = (freq_index[None, :] * window_pos[:, None] % twice_length).astype(
        jnp.float32
    ) * angle_unit
    parity = jnp.where(freq_index % 2 == 0, 1.0, -1.0).astype(jnp.float32)[:, None]
    return (
        jnp.cos(fwd_phase).astype(jnp.bfloat16),
        jnp.sin(fwd_phase).astype(jnp.bfloat16),
        jnp.cos(back_phase).astype(jnp.bfloat16),
        jnp.sin(back_phase).astype(jnp.bfloat16),
        jnp.cos(window_phase).astype(jnp.bfloat16),
        jnp.sin(window_phase).astype(jnp.bfloat16),
        parity,
    )


def spectra(block_list, cosine_forward, sine_forward):
    cosine_piece = jnp.einsum(
        "qk,rkb->rqb", cosine_forward, block_list, preferred_element_type=jnp.float32
    )
    sine_piece = jnp.einsum(
        "qk,rkb->rqb", sine_forward, block_list, preferred_element_type=jnp.float32
    )
    return (cosine_piece, sine_piece)


def shards(grad_out, out_weight, query_gate, key_branch, value_branch, filter_taps):
    seg_len = query_gate.shape[0]
    channels = query_gate.shape[1]
    twice_length = 2 * seg_len
    segments = lax.axis_size("seq")
    my_index = lax.axis_index("seq")
    factor = 1.0 / math.sqrt(seg_len * segments)
    grad_mix = lax.dot_general(
        lax.all_gather(grad_out, "ch", axis=1, tiled=True),
        out_weight,
        (((1,), (1,)), ((), ())),
        preferred_element_type=jnp.float32,
    )
    gated_grad = (grad_mix * query_gate.astype(jnp.float32)).astype(jnp.bfloat16)
    conv_input = (key_branch.astype(jnp.float32) * value_branch.astype(jnp.float32)).astype(
        jnp.bfloat16
    )
    tables = build_tables(seg_len)
    (
        cosine_forward,
        sine_forward,
        cosine_backward,
        sine_backward,
        cosine_window,
        sine_window,
        parity,
    ) = tables
    all_taps = lax.all_gather(filter_taps, "seq", axis=0, tiled=True)
    tap_cos, tap_sin = spectra(
        all_taps.reshape(segments, seg_len, channels), cosine_forward, sine_forward
    )
    kern_cos = jnp.concatenate([jnp.zeros_like(tap_cos[:1]), tap_cos[:-1]], 0) + parity * tap_cos
    kern_sin = jnp.concatenate([jnp.zeros_like(tap_sin[:1]), tap_sin[:-1]], 0) + parity * tap_sin
    own_cos, own_sin = spectra(conv_input[None], cosine_forward, sine_forward)
    own_cos = own_cos[0]
    own_sin = own_sin[0]
    zero_spec = jnp.zeros((twice_length, channels), jnp.float32)
    initial = (zero_spec, zero_spec, jnp.zeros(((segments + 1) * seg_len, channels), jnp.float32))
    piece_data = lax.all_gather(gated_grad, "seq", axis=0, tiled=True)
    block_count = piece_data.shape[0] // seg_len
    seg_ids = jnp.arange(block_count, dtype=jnp.int32)
    block_list = piece_data.reshape(block_count, seg_len, channels)
    grad_cos, grad_sin = spectra(block_list, cosine_forward, sine_forward)
    lag_steps = seg_ids - my_index
    inside = seg_ids < segments
    live_mask = ((lag_steps >= 0) & inside).astype(jnp.float32)[:, None, None]
    lag_clip = jnp.clip(lag_steps, 0, segments - 1)
    lag_kcos = jnp.take(kern_cos, lag_clip, axis=0)
    lag_ksin = jnp.take(kern_sin, lag_clip, axis=0)
    running_real = jnp.sum(live_mask * (grad_cos * lag_kcos + grad_sin * lag_ksin), axis=0)
    running_imaginary = jnp.sum(live_mask * (grad_sin * lag_kcos - grad_cos * lag_ksin), axis=0)
    product_real = (own_cos * grad_cos + own_sin * grad_sin).astype(jnp.bfloat16)
    product_imaginary = (own_sin * grad_cos - own_cos * grad_sin).astype(jnp.bfloat16)
    windows = jnp.einsum(
        "an,hny->hay", cosine_window, product_real, preferred_element_type=jnp.float32
    ) - jnp.einsum(
        "an,hny->hay", sine_window, product_imaginary, preferred_element_type=jnp.float32
    )
    windows = windows * (live_mask / twice_length)

    def place(item_index, buffer):
        offset = lag_clip[item_index] * seg_len
        current = lax.dynamic_slice_in_dim(buffer, offset, twice_length, 0)
        return lax.dynamic_update_slice_in_dim(buffer, current + windows[item_index], offset, 0)

    buffer = lax.fori_loop(0, block_list.shape[0], place, initial[2])
    convolution_gradient = (
        jnp.dot(
            cosine_backward, running_real.astype(jnp.bfloat16), preferred_element_type=jnp.float32
        )
        - jnp.dot(
            sine_backward,
            running_imaginary.astype(jnp.bfloat16),
            preferred_element_type=jnp.float32,
        )
    ) / twice_length
    own_rows = lax.psum_scatter(
        buffer[seg_len:].astype(jnp.bfloat16), "seq", scatter_dimension=0, tiled=True
    ).astype(jnp.float32)
    filter_grad = own_rows * factor
    key_grad = (convolution_gradient * value_branch.astype(jnp.float32)).astype(jnp.bfloat16)
    value_grad = (convolution_gradient * key_branch.astype(jnp.float32)).astype(jnp.bfloat16)
    return (key_grad, value_grad, filter_grad)


def half_tables(rows):
    size = 2 * rows
    freq = np.arange(rows)
    pos = np.arange(rows)
    angle = 2.0 * np.pi * (np.outer(freq, pos) % size) / size
    sine = np.sin(angle)
    sine[0] = (-1.0) ** pos
    forward = np.concatenate([np.cos(angle), sine], 0)
    angle = 2.0 * np.pi * (np.outer(rows - pos, freq) % size) / size
    cos_back = 2.0 * np.cos(angle)
    sin_back = -2.0 * np.sin(angle)
    cos_back[:, 0] = 1.0
    sin_back[:, 0] = (-1.0) ** (rows - pos)
    back = np.concatenate([cos_back, sin_back], 1) / size
    return forward.astype(ml_dtypes.bfloat16), back.astype(ml_dtypes.bfloat16)


ANY = pl.BlockSpec(memory_space=pl.ANY)
VMEM = pl.BlockSpec(memory_space=pltpu.VMEM)
MARK = jax.ShapeDtypeStruct((8, LANES), jnp.float32)


class Spot:
    def __init__(self):
        me, plane, planes = lax.axis_index("seq"), lax.axis_index("ch"), lax.axis_size("ch")
        low = plane < planes // 2
        self.chip, self.core = me // 2, me % 2
        self.outer = (plane == 0) | (plane == planes - 1)
        self.blocks = (plane, plane ^ 1, jnp.where(low, 2, 1), jnp.where(low, 3, 0))


def call(kernel, args, in_specs, outs, out_specs, name, scratch=(), limit=24, flops=0, update=(), carry=(), after=()):
    same = (*update, *carry)
    count, results, written = len(args), len(outs), len(outs) + len(update)

    def body(*refs):
        rest = refs[count + len(same) + len(after) :]
        mark, *scratch_refs = rest[results + len(same) :]
        mark[...] = jnp.zeros_like(mark)
        kernel(Spot(), *refs[:count], *rest[:written], *scratch_refs)

    return pl.pallas_call(
        body,
        input_output_aliases={count + i: results + i for i in range(len(same))},
        grid=(1,),
        in_specs=[*in_specs, *[ANY] * (len(same) + len(after))],
        out_specs=[*out_specs, *[ANY] * len(same), whole(MARK)],
        scratch_shapes=scratch,
        out_shape=[*outs, *[array(x.shape, x.dtype) for x in same], MARK],
        compiler_params=pltpu.CompilerParams(vmem_limit_bytes=limit * 2**20),
        cost_estimate=pl.CostEstimate(flops=flops, bytes_accessed=0, transcendentals=0),
        name=name,
    )(*args, *same, *after)


def whole(x):
    return pl.BlockSpec(x.shape, lambda *_: (0,) * len(x.shape))


def array(shape, dtype=jnp.bfloat16):
    return jax.ShapeDtypeStruct(shape, dtype)


def place(spot, k, core, width):
    return pl.multiple_of(((spot.chip ^ k) * 2 + core) * width, width)


def load_kernel(chips, spot, weight, held, sem):
    width = held.shape[1]
    depth = held.shape[2] // 4
    copies = []
    for b in range(4):
        at = pl.multiple_of(spot.blocks[b] * depth, depth)
        for k in range(chips):
            rows = pl.ds(place(spot, k, spot.core, width), width)
            copies.append(
                pltpu.make_async_copy(
                    weight.at[rows, pl.ds(at, depth)],
                    held.at[k, :, pl.ds(b * depth, depth)],
                    sem.at[b * chips + k],
                )
            )
    for copy in copies:
        copy.start()
    for copy in copies:
        copy.wait()


def load(weight, chips, **order):
    held = (chips, weight.shape[0] // (2 * chips), weight.shape[1])
    return call(
        functools.partial(load_kernel, chips),
        (weight,),
        [ANY],
        [pltpu.VMEM(held, weight.dtype)],
        [VMEM],
        "load_weight",
        [pltpu.SemaphoreType.DMA((4 * chips,))],
        **order,
    )


def pack_kernel(chips, spot, gate, key, value, taps, mine, theirs_0, theirs_1, all_in, sem):
    width = mine.shape[3]
    half = theirs_0.shape[2]
    loads = [pltpu.make_async_copy(ref, all_in.at[i], sem.at[i]) for i, ref in enumerate((gate, taps, key, value))]
    for copy in loads:
        copy.start()
    for copy in loads:
        copy.wait()
    upper, lower = slice(0, half), slice(half, 2 * half)
    for out, core, rows in (
        (theirs_0, 1 - spot.core, upper),
        (theirs_1, 1 - spot.core, lower),
        (mine, spot.core, slice(None)),
    ):
        for k in range(chips):
            here = (rows, pl.ds(place(spot, k, core, width), width))
            out[0, k] = all_in[(0, *here)]
            out[1, k] = all_in[(1, *here)]
            product = all_in[(2, *here)].astype(jnp.float32) * all_in[(3, *here)].astype(jnp.float32)
            out[2, k] = product.astype(jnp.bfloat16)


def pack(gate, key, value, taps, chips, **order):
    rows, channels = key.shape
    out = (3, chips, rows, channels // (2 * chips))
    half = array((3, chips, rows // 2, channels // (2 * chips)))
    return call(
        functools.partial(pack_kernel, chips),
        (gate, key, value, taps),
        [ANY] * 4,
        [pltpu.VMEM(out, jnp.bfloat16), half, half],
        [VMEM, whole(half), whole(half)],
        "pack_core",
        [pltpu.VMEM((4, rows, channels), jnp.bfloat16), pltpu.SemaphoreType.DMA((4,))],
        limit=58,
        **order,
    )


def merge_kernel(spot, mine, other_0, other_1, gates, *refs):
    *outs, sem = refs
    own, theirs = spot.core, 1 - spot.core
    half = other_0.shape[2]
    loads = []
    for h, other in enumerate((other_0, other_1)):
        rows = pl.ds(h * half, half)
        for k, out in enumerate(outs):
            for i, to in enumerate((gates.at[k, 1, rows], out.at[0, theirs, rows], out.at[1, theirs, rows])):
                loads.append(pltpu.make_async_copy(other.at[i, k], to, sem.at[len(loads)]))
    for copy in loads:
        copy.start()
    for k, out in enumerate(outs):
        gates[k, 0] = mine[0, k]
        out[0, own] = mine[1, k]
        out[1, own] = mine[2, k]
    for copy in loads:
        copy.wait()


def merge(mine, others, **order):
    _, chips, rows, width = mine.shape
    piece = array((2, 2, rows, width))
    out = call(
        merge_kernel,
        (mine, *others),
        [VMEM, ANY, ANY],
        [pltpu.VMEM((chips, 2, rows, width), jnp.bfloat16)] + [piece] * chips,
        [VMEM] + [whole(piece)] * chips,
        "merge_cores",
        [pltpu.SemaphoreType.DMA((6 * chips,))],
        **order,
    )
    return out[0], out[1 : 1 + chips], out[1 + chips :]


def contract(x, w):
    return lax.dot_general(x, w, (((1,), (1,)), ((), ())), preferred_element_type=jnp.float32)


def fetch(spot, groups, x, sem):
    rows = groups[0][0].shape[0]
    for i, group in enumerate(groups):
        to = x.at[pl.ds(i * rows, rows)]
        for j, ref in enumerate(group):
            copy = pltpu.make_async_copy(ref, to, sem.at[i])
            if len(group) == 1:
                copy.start()
            else:
                pl.when(spot.outer if j == 0 else ~spot.outer)(copy.start)
    for i, group in enumerate(groups):
        pltpu.make_async_copy(group[0], x.at[pl.ds(i * rows, rows)], sem.at[i]).wait()


def grouped(refs, sizes):
    refs = list(refs)
    return [[refs.pop(0) for _ in range(s)] for s in sizes]


def mix_kernel(block, sizes, has_total, spot, *refs):
    count = sum(sizes)
    groups = grouped(refs[:count], sizes)
    held, *rest = refs[count:]
    total, out, x, sem = rest if has_total else (None, *rest)
    depth = x.shape[1]
    fetch(spot, groups, x, sem)

    @pl.loop(0, held.shape[0])
    def _(k):
        value = contract(x[...], held[k, :, block * depth : (block + 1) * depth])
        out[k] = value + total[k] if has_total else value


def mix(block, groups, held, total, **order):
    chips, width, _ = held.shape
    sizes = [len(g) for g in groups]
    flat = [x for g in groups for x in g]
    rows = sum(g[0].shape[0] for g in groups)
    depth = flat[0].shape[1]
    out = (chips, rows, width)
    return call(
        functools.partial(mix_kernel, block, sizes, total is not None),
        (*flat, held) + ((total,) if total is not None else ()),
        [ANY] * len(flat) + [VMEM] + ([VMEM] if total is not None else []),
        [pltpu.VMEM(out, jnp.float32)],
        [VMEM],
        "mix",
        [pltpu.VMEM((rows, depth), jnp.bfloat16), pltpu.SemaphoreType.DMA((len(groups),))],
        **order,
    )


def gate_kernel(sizes, spot, *refs):
    count = sum(sizes)
    groups = grouped(refs[:count], sizes)
    held, total, gates, *outs, x, sem = refs[count:]
    depth = x.shape[1]
    rows = x.shape[0] // 2
    fetch(spot, groups, x, sem)
    for k, out in enumerate(outs):
        value = contract(x[...], held[k, :, 3 * depth : 4 * depth])
        for h, core in enumerate((spot.core, 1 - spot.core)):
            own = slice(h * rows, (h + 1) * rows)
            mixed = total[k, own] + value[own]
            out[core] = (mixed * gates[k, h].astype(jnp.float32)).astype(jnp.bfloat16)


def mix_gate(groups, held, total, gates):
    chips, width, _ = held.shape
    sizes = [len(g) for g in groups]
    flat = [x for g in groups for x in g]
    rows, depth = flat[0].shape
    piece = array((2, rows, width))
    return call(
        functools.partial(gate_kernel, sizes),
        (*flat, held, total, gates),
        [ANY] * len(flat) + [VMEM] * 3,
        [piece] * chips,
        [whole(piece)] * chips,
        "mix_gate",
        [pltpu.VMEM((2 * rows, depth), jnp.bfloat16), pltpu.SemaphoreType.DMA((len(groups),))],
    )


def tap_kernel(spot, forward, *refs):
    *pieces, out, spec = refs
    segs = len(pieces)
    seg = forward.shape[1]
    width = pieces[0].shape[3]
    row = lax.broadcasted_iota(jnp.int32, (2 * seg, width), 0)
    sign = jnp.where(row % 2 == 0, 1.0, -1.0)
    for x in range(2):
        for k, piece in enumerate(pieces):
            block = piece[x].reshape(seg, width)
            spec[spot.chip ^ k] = jnp.dot(forward[...], block, preferred_element_type=jnp.float32)
        for r in range(segs):
            kern = sign * spec[r]
            if r:
                kern += spec[r - 1]
            out[x, r] = kern.astype(jnp.bfloat16)


def tap_kernels(forward, pieces, **order):
    segs = len(pieces)
    width = pieces[0].shape[3]
    shape = (2, segs, *forward.shape[:1], width)
    return call(
        tap_kernel,
        (forward, *pieces),
        [whole(forward)] + [whole(p) for p in pieces],
        [pltpu.VMEM(shape, jnp.bfloat16)],
        [VMEM],
        "kernels",
        [pltpu.VMEM(shape[1:], jnp.float32)],
        flops=12 * math.prod(shape) * forward.shape[1],
        **order,
    )


def correlate_kernel(parts, spot, forward, back, kern, *refs):
    segs = kern.shape[1]
    n = 2 * segs
    pieces = refs[: segs * parts]
    outs = refs[segs * parts : segs * parts + n]
    data, spec, acc, result = refs[segs * parts + n :]
    part = pieces[0].shape[1]
    rows = part * parts
    seg = 2 * rows
    width = data.shape[2]
    for k in range(segs):
        for c in range(parts):
            for core in range(2):
                at = core * rows + c * part
                data[spot.chip ^ k, at : at + part] = pieces[k * parts + c][core]
    for i in range(segs):
        spec[i] = jnp.dot(forward[...], data[i], preferred_element_type=jnp.float32)

    tile = 16

    def products(x, row, lane, first):
        here = (pl.ds(row, tile), pl.ds(lane, LANES))
        there = (pl.ds(row + seg, tile), pl.ds(lane, LANES))
        g_real = [spec[(i, *here)] for i in range(segs)]
        g_imag = [spec[(i, *there)] for i in range(segs)]
        k_real = [kern[(x, r, *here)].astype(jnp.float32) for r in range(segs)]
        k_imag = [kern[(x, r, *there)].astype(jnp.float32) for r in range(segs)]
        if first:
            edge = lax.broadcasted_iota(jnp.int32, (tile, LANES), 0) == 0
        for j in range(segs):
            both = sum(g_real[i] * k_real[i - j] for i in range(j, segs))
            other = sum(g_imag[i] * k_imag[i - j] for i in range(j, segs))
            cross = sum(g_imag[i] * k_real[i - j] - g_real[i] * k_imag[i - j] for i in range(j, segs))
            if first:
                real = both + jnp.where(edge, 0.0, other)
                cross = jnp.where(edge, other, cross)
            else:
                real = both + other
            acc[(j, *here)] = real.astype(jnp.bfloat16)
            acc[(j, *there)] = cross.astype(jnp.bfloat16)

    for x in range(2):
        for lane in range(0, width, LANES):
            products(x, 0, lane, True)

            @pl.loop(1, seg // tile, unroll=seg // tile - 1)
            def _(t):
                products(x, pl.multiple_of(t * tile, tile), lane, False)

        for j in range(segs):
            value = jnp.dot(back[...], acc[j], preferred_element_type=jnp.float32).astype(jnp.bfloat16)
            for core in range(2):
                result[2 * j + core, x] = value[core * rows : (core + 1) * rows]
    me = 2 * spot.chip + spot.core
    for k in range(n):
        outs[k][...] = result[me ^ k]


def correlate(forward, back, kern, pieces):
    segs, parts = len(pieces), len(pieces[0])
    flat = [p for group in pieces for p in group]
    width = flat[0].shape[2]
    rows = flat[0].shape[1] * parts
    seg = 2 * rows
    n = 2 * segs
    out = array((2, rows, width))
    return call(
        functools.partial(correlate_kernel, parts),
        (forward, back, kern, *flat),
        [whole(forward), whole(back), VMEM] + [whole(p) for p in flat],
        [out] * n,
        [whole(out)] * n,
        "correlate",
        [
            pltpu.VMEM((segs, seg, width), jnp.bfloat16),
            pltpu.VMEM((segs, 2 * seg, width), jnp.float32),
            pltpu.VMEM((segs, 2 * seg, width), jnp.bfloat16),
            pltpu.VMEM((n, *out.shape), jnp.bfloat16),
        ],
    )


def finish_kernel(ks, factor, fetch_branches, spot, *refs):
    n = len(ks)
    if fetch_branches:
        (key, value, *pieces), refs = refs[: 2 + n], refs[2 + n :]
        branches, *outs, piece_v, key_o, value_o, filter_o, in_sem, out_sem = refs
    else:
        (branches, *pieces), refs = refs[: 1 + n], refs[1 + n :]
        *outs, piece_v, key_o, value_o, filter_o, in_sem, out_sem = refs
    width = piece_v.shape[3]
    me = 2 * spot.chip + spot.core
    loads = [pltpu.make_async_copy(p, piece_v.at[i], in_sem.at[i]) for i, p in enumerate(pieces)]
    if fetch_branches:
        loads.append(pltpu.make_async_copy(key, branches.at[0], in_sem.at[n]))
        loads.append(pltpu.make_async_copy(value, branches.at[1], in_sem.at[n + 1]))
    for copy in loads:
        copy.start()
    for copy in loads:
        copy.wait()
    stores = []
    for i, k in enumerate(ks):
        here = (slice(None), pl.ds(pl.multiple_of((me ^ k) * width, width), width))
        conv_grad = piece_v[i, 0].astype(jnp.float32)
        key_o[i] = (conv_grad * branches[(1, *here)].astype(jnp.float32)).astype(jnp.bfloat16)
        value_o[i] = (conv_grad * branches[(0, *here)].astype(jnp.float32)).astype(jnp.bfloat16)
        filter_o[i] = piece_v[i, 1].astype(jnp.float32) * factor
        for o, (src, dst) in enumerate(zip((key_o, value_o, filter_o), outs)):
            stores.append(pltpu.make_async_copy(src.at[i], dst.at[here], out_sem.at[o, i]))
            stores[-1].start()
    for copy in stores:
        copy.wait()


def finish(ks, pieces, factor, key=None, value=None, branches=None, grads=None):
    begin = branches is None
    n = len(ks)
    rows, width = pieces[0].shape[1:]
    scratch = [
        pltpu.VMEM((n, 2, rows, width), jnp.bfloat16),
        pltpu.VMEM((n, rows, width), jnp.bfloat16),
        pltpu.VMEM((n, rows, width), jnp.bfloat16),
        pltpu.VMEM((n, rows, width), jnp.float32),
        pltpu.SemaphoreType.DMA((n + 2,)),
        pltpu.SemaphoreType.DMA((3, n)),
    ]
    kernel = functools.partial(finish_kernel, ks, factor, begin)
    if begin:
        both = pltpu.VMEM((2, *key.shape), key.dtype)
        outs = [both, array(key.shape), array(key.shape), array(key.shape, jnp.float32)]
        args = (key, value, *pieces)
        return call(kernel, args, [ANY] * len(args), outs, [VMEM, *[ANY] * 3], "finish", scratch)
    args = (branches, *pieces)
    return call(kernel, args, [VMEM, *[ANY] * n], [], [], "finish", scratch, update=grads)


def hold(arrays, after):
    return call(lambda spot: None, (), [], [], [], "hold", carry=arrays, after=after)


def swap(x, k, n):
    return lax.ppermute(x, "seq", [(i, i ^ k) for i in range(n)]) if k else x


def fast_shards(grad_out, out_weight, query_gate, key_branch, value_branch, filter_taps):
    n = lax.axis_size("seq")
    planes = lax.axis_size("ch")
    rows = grad_out.shape[0]
    chips = n // 2
    factor = 1.0 / math.sqrt(rows * n)
    forward, back = (jnp.asarray(t) for t in half_tables(2 * rows))
    outer = [(i, i ^ 1) for i in range(planes)]
    inner = []
    for s in range(n):
        inner += [(s * planes + 1, s * planes + 2), (s * planes + 2, s * planes + 1)]
        inner += [(s * planes + z, (s ^ 1) * planes + z) for z in (0, planes - 1)]

    def send_outer(x):
        return lax.ppermute(x, "ch", outer)

    def send_inner(x):
        return lax.ppermute(x, ("seq", "ch"), inner)

    def other(x):
        return swap(x, 1, n)

    outer_0, inner_0, others = send_outer(grad_out), send_inner(grad_out), other(grad_out)
    mine, *packed, packed_mark = pack(query_gate, key_branch, value_branch, filter_taps, chips)
    gates, taps_input, (merged,) = merge(mine, [other(x) for x in packed], after=[packed_mark])
    taps_input = [swap(x, 2 * k, n) for k, x in enumerate(taps_input)]
    outer_1, inner_1 = send_outer(inner_0), send_inner(outer_0)
    held, loaded = load(out_weight, chips, after=[merged])
    total, first = mix(0, [[grad_out], [others]], held, None, after=[loaded])
    kern, tapped = tap_kernels(forward, taps_input, after=[first])
    outer_1, inner_1, gone = hold([outer_1, inner_1], after=[tapped])
    outer_2 = send_outer(inner_1)
    total, outer_1, second = mix(1, [[outer_0], [other(outer_0)]], held, total, carry=[outer_1], after=[gone])
    blocks = [[outer_1, inner_0], [other(outer_1), other(inner_0)]]
    total, _ = mix(2, blocks, held, total, after=[second])
    gated = mix_gate([[outer_2, inner_1], [other(outer_2), other(inner_1)]], held, total, gates)[:chips]
    gated = [[swap(p, 2 * k, n)] for k, p in enumerate(gated)]

    results = correlate(forward, back, kern, gated)[:n]
    order = sorted(range(n), key=lambda k: ((k // 2).bit_count(), k % 2, k))
    results = {k: swap(results[k], k, n) for k in order}
    near, far = order[: n // 2], order[n // 2 :]
    branches, *grads, _ = finish(near, [results[k] for k in near], factor, key=key_branch, value=value_branch)
    return tuple(finish(far, [results[k] for k in far], factor, branches=branches, grads=grads)[:3])


def solution(mesh):
    specs = dict(
        mesh=mesh,
        in_specs=(
            P("seq", "ch"),
            P("ch", None),
            P("seq", "ch"),
            P("seq", "ch"),
            P("seq", "ch"),
            P("seq", "ch"),
        ),
        out_specs=(P("seq", "ch"), P("seq", "ch"), P("seq", "ch")),
        check_vma=False,
    )
    n, planes = mesh.shape["seq"], mesh.shape["ch"]

    def step(*arrays):
        whole_tiles = arrays[1].shape[0] // planes % (n * LANES) == 0
        fits = whole_tiles and planes == 4 and n & (n - 1) == 0
        return jax.shard_map(fast_shards if fits else shards, **specs)(*arrays)

    return step
```

```python
import functools
import math

import jax
import jax.numpy as jnp
import ml_dtypes
import numpy as np
from jax import lax
from jax.experimental import pallas as pl
from jax.experimental.pallas import tpu as pltpu
from jax.sharding import PartitionSpec as P

LANES = 128


def build_tables(seg_len):
    twice_length = 2 * seg_len
    freq_index = jnp.arange(twice_length, dtype=jnp.int32)
    row_index = jnp.arange(seg_len, dtype=jnp.int32)
    angle_unit = 2.0 * math.pi / twice_length
    fwd_phase = (freq_index[:, None] * row_index[None, :] % twice_length).astype(
        jnp.float32
    ) * angle_unit
    back_phase = (freq_index[None, :] * (seg_len - row_index[:, None]) % twice_length).astype(
        jnp.float32
    ) * angle_unit
    window_pos = (freq_index + seg_len) % twice_length
    window_phase = (freq_index[None, :] * window_pos[:, None] % twice_length).astype(
        jnp.float32
    ) * angle_unit
    parity = jnp.where(freq_index % 2 == 0, 1.0, -1.0).astype(jnp.float32)[:, None]
    return (
        jnp.cos(fwd_phase).astype(jnp.bfloat16),
        jnp.sin(fwd_phase).astype(jnp.bfloat16),
        jnp.cos(back_phase).astype(jnp.bfloat16),
        jnp.sin(back_phase).astype(jnp.bfloat16),
        jnp.cos(window_phase).astype(jnp.bfloat16),
        jnp.sin(window_phase).astype(jnp.bfloat16),
        parity,
    )


def spectra(block_list, cosine_forward, sine_forward):
    cosine_piece = jnp.einsum(
        "qk,rkb->rqb", cosine_forward, block_list, preferred_element_type=jnp.float32
    )
    sine_piece = jnp.einsum(
        "qk,rkb->rqb", sine_forward, block_list, preferred_element_type=jnp.float32
    )
    return (cosine_piece, sine_piece)


def shards(grad_out, out_weight, query_gate, key_branch, value_branch, filter_taps):
    seg_len = query_gate.shape[0]
    channels = query_gate.shape[1]
    twice_length = 2 * seg_len
    segments = lax.axis_size("seq")
    my_index = lax.axis_index("seq")
    factor = 1.0 / math.sqrt(seg_len * segments)
    grad_mix = lax.dot_general(
        lax.all_gather(grad_out, "ch", axis=1, tiled=True),
        out_weight,
        (((1,), (1,)), ((), ())),
        preferred_element_type=jnp.float32,
    )
    gated_grad = (grad_mix * query_gate.astype(jnp.float32)).astype(jnp.bfloat16)
    conv_input = (key_branch.astype(jnp.float32) * value_branch.astype(jnp.float32)).astype(
        jnp.bfloat16
    )
    tables = build_tables(seg_len)
    (
        cosine_forward,
        sine_forward,
        cosine_backward,
        sine_backward,
        cosine_window,
        sine_window,
        parity,
    ) = tables
    all_taps = lax.all_gather(filter_taps, "seq", axis=0, tiled=True)
    tap_cos, tap_sin = spectra(
        all_taps.reshape(segments, seg_len, channels), cosine_forward, sine_forward
    )
    kern_cos = jnp.concatenate([jnp.zeros_like(tap_cos[:1]), tap_cos[:-1]], 0) + parity * tap_cos
    kern_sin = jnp.concatenate([jnp.zeros_like(tap_sin[:1]), tap_sin[:-1]], 0) + parity * tap_sin
    own_cos, own_sin = spectra(conv_input[None], cosine_forward, sine_forward)
    own_cos = own_cos[0]
    own_sin = own_sin[0]
    zero_spec = jnp.zeros((twice_length, channels), jnp.float32)
    initial = (zero_spec, zero_spec, jnp.zeros(((segments + 1) * seg_len, channels), jnp.float32))
    piece_data = lax.all_gather(gated_grad, "seq", axis=0, tiled=True)
    block_count = piece_data.shape[0] // seg_len
    seg_ids = jnp.arange(block_count, dtype=jnp.int32)
    block_list = piece_data.reshape(block_count, seg_len, channels)
    grad_cos, grad_sin = spectra(block_list, cosine_forward, sine_forward)
    lag_steps = seg_ids - my_index
    inside = seg_ids < segments
    live_mask = ((lag_steps >= 0) & inside).astype(jnp.float32)[:, None, None]
    lag_clip = jnp.clip(lag_steps, 0, segments - 1)
    lag_kcos = jnp.take(kern_cos, lag_clip, axis=0)
    lag_ksin = jnp.take(kern_sin, lag_clip, axis=0)
    running_real = jnp.sum(live_mask * (grad_cos * lag_kcos + grad_sin * lag_ksin), axis=0)
    running_imaginary = jnp.sum(live_mask * (grad_sin * lag_kcos - grad_cos * lag_ksin), axis=0)
    product_real = (own_cos * grad_cos + own_sin * grad_sin).astype(jnp.bfloat16)
    product_imaginary = (own_sin * grad_cos - own_cos * grad_sin).astype(jnp.bfloat16)
    windows = jnp.einsum(
        "an,hny->hay", cosine_window, product_real, preferred_element_type=jnp.float32
    ) - jnp.einsum(
        "an,hny->hay", sine_window, product_imaginary, preferred_element_type=jnp.float32
    )
    windows = windows * (live_mask / twice_length)

    def place(item_index, buffer):
        offset = lag_clip[item_index] * seg_len
        current = lax.dynamic_slice_in_dim(buffer, offset, twice_length, 0)
        return lax.dynamic_update_slice_in_dim(buffer, current + windows[item_index], offset, 0)

    buffer = lax.fori_loop(0, block_list.shape[0], place, initial[2])
    convolution_gradient = (
        jnp.dot(
            cosine_backward, running_real.astype(jnp.bfloat16), preferred_element_type=jnp.float32
        )
        - jnp.dot(
            sine_backward,
            running_imaginary.astype(jnp.bfloat16),
            preferred_element_type=jnp.float32,
        )
    ) / twice_length
    own_rows = lax.psum_scatter(
        buffer[seg_len:].astype(jnp.bfloat16), "seq", scatter_dimension=0, tiled=True
    ).astype(jnp.float32)
    filter_grad = own_rows * factor
    key_grad = (convolution_gradient * value_branch.astype(jnp.float32)).astype(jnp.bfloat16)
    value_grad = (convolution_gradient * key_branch.astype(jnp.float32)).astype(jnp.bfloat16)
    return (key_grad, value_grad, filter_grad)


def half_tables(rows):
    size = 2 * rows
    freq = np.arange(rows)
    pos = np.arange(rows)
    angle = 2.0 * np.pi * (np.outer(freq, pos) % size) / size
    sine = np.sin(angle)
    sine[0] = (-1.0) ** pos
    forward = np.concatenate([np.cos(angle), sine], 0)
    angle = 2.0 * np.pi * (np.outer(rows - pos, freq) % size) / size
    cos_back = 2.0 * np.cos(angle)
    sin_back = -2.0 * np.sin(angle)
    cos_back[:, 0] = 1.0
    sin_back[:, 0] = (-1.0) ** (rows - pos)
    back = np.concatenate([cos_back, sin_back], 1) / size
    return forward.astype(ml_dtypes.bfloat16), back.astype(ml_dtypes.bfloat16)


ANY = pl.BlockSpec(memory_space=pl.ANY)
VMEM = pl.BlockSpec(memory_space=pltpu.VMEM)
MARK = jax.ShapeDtypeStruct((8, LANES), jnp.float32)


class Spot:
    def __init__(self):
        me, plane, planes = lax.axis_index("seq"), lax.axis_index("ch"), lax.axis_size("ch")
        low = plane < planes // 2
        self.chip, self.core = me // 2, me % 2
        self.outer = (plane == 0) | (plane == planes - 1)
        self.blocks = (plane, plane ^ 1, jnp.where(low, 2, 1), jnp.where(low, 3, 0))


def call(kernel, args, in_specs, outs, out_specs, name, scratch=(), limit=24, flops=0, update=(), carry=(), after=()):
    same = (*update, *carry)
    count, results, written = len(args), len(outs), len(outs) + len(update)

    def body(*refs):
        rest = refs[count + len(same) + len(after) :]
        mark, *scratch_refs = rest[results + len(same) :]
        mark[...] = jnp.zeros_like(mark)
        kernel(Spot(), *refs[:count], *rest[:written], *scratch_refs)

    return pl.pallas_call(
        body,
        input_output_aliases={count + i: results + i for i in range(len(same))},
        grid=(1,),
        in_specs=[*in_specs, *[ANY] * (len(same) + len(after))],
        out_specs=[*out_specs, *[ANY] * len(same), whole(MARK)],
        scratch_shapes=scratch,
        out_shape=[*outs, *[array(x.shape, x.dtype) for x in same], MARK],
        compiler_params=pltpu.CompilerParams(vmem_limit_bytes=limit * 2**20),
        cost_estimate=pl.CostEstimate(flops=flops, bytes_accessed=0, transcendentals=0),
        name=name,
    )(*args, *same, *after)


def whole(x):
    return pl.BlockSpec(x.shape, lambda *_: (0,) * len(x.shape))


def array(shape, dtype=jnp.bfloat16):
    return jax.ShapeDtypeStruct(shape, dtype)


def place(spot, k, core, width):
    return pl.multiple_of(((spot.chip ^ k) * 2 + core) * width, width)


def load_kernel(chips, spot, weight, held, sem):
    width = held.shape[1]
    depth = held.shape[2] // 4
    copies = []
    for b in range(4):
        at = pl.multiple_of(spot.blocks[b] * depth, depth)
        for k in range(chips):
            rows = pl.ds(place(spot, k, spot.core, width), width)
            copies.append(
                pltpu.make_async_copy(
                    weight.at[rows, pl.ds(at, depth)],
                    held.at[k, :, pl.ds(b * depth, depth)],
                    sem.at[b * chips + k],
                )
            )
    for copy in copies:
        copy.start()
    for copy in copies:
        copy.wait()


def load(weight, chips, **order):
    held = (chips, weight.shape[0] // (2 * chips), weight.shape[1])
    return call(
        functools.partial(load_kernel, chips),
        (weight,),
        [ANY],
        [pltpu.VMEM(held, weight.dtype)],
        [VMEM],
        "load_weight",
        [pltpu.SemaphoreType.DMA((4 * chips,))],
        **order,
    )


def pack_kernel(chips, spot, gate, key, value, taps, mine, theirs_0, theirs_1, all_in, sem):
    width = mine.shape[3]
    half = theirs_0.shape[2]
    loads = [pltpu.make_async_copy(ref, all_in.at[i], sem.at[i]) for i, ref in enumerate((gate, taps, key, value))]
    for copy in loads:
        copy.start()
    for copy in loads:
        copy.wait()
    upper, lower = slice(0, half), slice(half, 2 * half)
    for out, core, rows in (
        (theirs_0, 1 - spot.core, upper),
        (theirs_1, 1 - spot.core, lower),
        (mine, spot.core, slice(None)),
    ):
        for k in range(chips):
            here = (rows, pl.ds(place(spot, k, core, width), width))
            out[0, k] = all_in[(0, *here)]
            out[1, k] = all_in[(1, *here)]
            product = all_in[(2, *here)].astype(jnp.float32) * all_in[(3, *here)].astype(jnp.float32)
            out[2, k] = product.astype(jnp.bfloat16)


def pack(gate, key, value, taps, chips, **order):
    rows, channels = key.shape
    out = (3, chips, rows, channels // (2 * chips))
    half = array((3, chips, rows // 2, channels // (2 * chips)))
    return call(
        functools.partial(pack_kernel, chips),
        (gate, key, value, taps),
        [ANY] * 4,
        [pltpu.VMEM(out, jnp.bfloat16), half, half],
        [VMEM, whole(half), whole(half)],
        "pack_core",
        [pltpu.VMEM((4, rows, channels), jnp.bfloat16), pltpu.SemaphoreType.DMA((4,))],
        limit=58,
        **order,
    )


def merge_kernel(spot, mine, other_0, other_1, gates, *refs):
    *outs, sem = refs
    own, theirs = spot.core, 1 - spot.core
    half = other_0.shape[2]
    loads = []
    for h, other in enumerate((other_0, other_1)):
        rows = pl.ds(h * half, half)
        for k, out in enumerate(outs):
            for i, to in enumerate((gates.at[k, 1, rows], out.at[0, theirs, rows], out.at[1, theirs, rows])):
                loads.append(pltpu.make_async_copy(other.at[i, k], to, sem.at[len(loads)]))
    for copy in loads:
        copy.start()
    for k, out in enumerate(outs):
        gates[k, 0] = mine[0, k]
        out[0, own] = mine[1, k]
        out[1, own] = mine[2, k]
    for copy in loads:
        copy.wait()


def merge(mine, others, **order):
    _, chips, rows, width = mine.shape
    piece = array((2, 2, rows, width))
    out = call(
        merge_kernel,
        (mine, *others),
        [VMEM, ANY, ANY],
        [pltpu.VMEM((chips, 2, rows, width), jnp.bfloat16)] + [piece] * chips,
        [VMEM] + [whole(piece)] * chips,
        "merge_cores",
        [pltpu.SemaphoreType.DMA((6 * chips,))],
        **order,
    )
    return out[0], out[1 : 1 + chips], out[1 + chips :]


def contract(x, w):
    return lax.dot_general(x, w, (((1,), (1,)), ((), ())), preferred_element_type=jnp.float32)


def fetch(spot, groups, x, sem):
    rows = groups[0][0].shape[0]
    for i, group in enumerate(groups):
        to = x.at[pl.ds(i * rows, rows)]
        for j, ref in enumerate(group):
            copy = pltpu.make_async_copy(ref, to, sem.at[i])
            if len(group) == 1:
                copy.start()
            else:
                pl.when(spot.outer if j == 0 else ~spot.outer)(copy.start)
    for i, group in enumerate(groups):
        pltpu.make_async_copy(group[0], x.at[pl.ds(i * rows, rows)], sem.at[i]).wait()


def grouped(refs, sizes):
    refs = list(refs)
    return [[refs.pop(0) for _ in range(s)] for s in sizes]


def mix_kernel(block, sizes, has_total, spot, *refs):
    count = sum(sizes)
    groups = grouped(refs[:count], sizes)
    held, *rest = refs[count:]
    total, out, x, sem = rest if has_total else (None, *rest)
    depth = x.shape[1]
    fetch(spot, groups, x, sem)

    @pl.loop(0, held.shape[0])
    def _(k):
        value = contract(x[...], held[k, :, block * depth : (block + 1) * depth])
        out[k] = value + total[k] if has_total else value


def mix(block, groups, held, total, **order):
    chips, width, _ = held.shape
    sizes = [len(g) for g in groups]
    flat = [x for g in groups for x in g]
    rows = sum(g[0].shape[0] for g in groups)
    depth = flat[0].shape[1]
    out = (chips, rows, width)
    return call(
        functools.partial(mix_kernel, block, sizes, total is not None),
        (*flat, held) + ((total,) if total is not None else ()),
        [ANY] * len(flat) + [VMEM] + ([VMEM] if total is not None else []),
        [pltpu.VMEM(out, jnp.float32)],
        [VMEM],
        "mix",
        [pltpu.VMEM((rows, depth), jnp.bfloat16), pltpu.SemaphoreType.DMA((len(groups),))],
        **order,
    )


def gate_kernel(sizes, spot, *refs):
    count = sum(sizes)
    groups = grouped(refs[:count], sizes)
    held, total, gates, *outs, x, sem = refs[count:]
    depth = x.shape[1]
    rows = x.shape[0] // 2
    fetch(spot, groups, x, sem)
    for k, out in enumerate(outs):
        value = contract(x[...], held[k, :, 3 * depth : 4 * depth])
        for h, core in enumerate((spot.core, 1 - spot.core)):
            own = slice(h * rows, (h + 1) * rows)
            mixed = total[k, own] + value[own]
            out[core] = (mixed * gates[k, h].astype(jnp.float32)).astype(jnp.bfloat16)


def mix_gate(groups, held, total, gates):
    chips, width, _ = held.shape
    sizes = [len(g) for g in groups]
    flat = [x for g in groups for x in g]
    rows, depth = flat[0].shape
    piece = array((2, rows, width))
    return call(
        functools.partial(gate_kernel, sizes),
        (*flat, held, total, gates),
        [ANY] * len(flat) + [VMEM] * 3,
        [piece] * chips,
        [whole(piece)] * chips,
        "mix_gate",
        [pltpu.VMEM((2 * rows, depth), jnp.bfloat16), pltpu.SemaphoreType.DMA((len(groups),))],
    )


def tap_kernel(spot, forward, *refs):
    *pieces, out, spec = refs
    segs = len(pieces)
    seg = forward.shape[1]
    width = pieces[0].shape[3]
    row = lax.broadcasted_iota(jnp.int32, (2 * seg, width), 0)
    sign = jnp.where(row % 2 == 0, 1.0, -1.0)
    for x in range(2):
        for k, piece in enumerate(pieces):
            block = piece[x].reshape(seg, width)
            spec[spot.chip ^ k] = jnp.dot(forward[...], block, preferred_element_type=jnp.float32)
        for r in range(segs):
            kern = sign * spec[r]
            if r:
                kern += spec[r - 1]
            out[x, r] = kern.astype(jnp.bfloat16)


def tap_kernels(forward, pieces, **order):
    segs = len(pieces)
    width = pieces[0].shape[3]
    shape = (2, segs, *forward.shape[:1], width)
    return call(
        tap_kernel,
        (forward, *pieces),
        [whole(forward)] + [whole(p) for p in pieces],
        [pltpu.VMEM(shape, jnp.bfloat16)],
        [VMEM],
        "kernels",
        [pltpu.VMEM(shape[1:], jnp.float32)],
        flops=12 * math.prod(shape) * forward.shape[1],
        **order,
    )


def correlate_kernel(ks, spot, forward, back, kern, *refs):
    segs = kern.shape[1]
    n = 2 * segs
    pieces = refs[:segs]
    outs = refs[segs : segs + n]
    data, spec, acc, result = refs[segs + n :]
    rows = pieces[0].shape[1]
    seg = 2 * rows
    width = data.shape[2]
    for k, piece in zip(ks, pieces):
        for core in range(2):
            data[spot.chip ^ k, core * rows : (core + 1) * rows] = piece[core]
    for i in range(segs):
        spec[i] = jnp.dot(forward[...], data[i], preferred_element_type=jnp.float32)

    tile = 16

    def products(x, row, lane, first):
        here = (pl.ds(row, tile), pl.ds(lane, LANES))
        there = (pl.ds(row + seg, tile), pl.ds(lane, LANES))
        g_real = [spec[(i, *here)] for i in range(segs)]
        g_imag = [spec[(i, *there)] for i in range(segs)]
        k_real = [kern[(x, r, *here)].astype(jnp.float32) for r in range(segs)]
        k_imag = [kern[(x, r, *there)].astype(jnp.float32) for r in range(segs)]
        if first:
            edge = lax.broadcasted_iota(jnp.int32, (tile, LANES), 0) == 0
        for j in range(segs):
            both = sum(g_real[i] * k_real[i - j] for i in range(j, segs))
            other = sum(g_imag[i] * k_imag[i - j] for i in range(j, segs))
            cross = sum(g_imag[i] * k_real[i - j] - g_real[i] * k_imag[i - j] for i in range(j, segs))
            if first:
                real = both + jnp.where(edge, 0.0, other)
                cross = jnp.where(edge, other, cross)
            else:
                real = both + other
            acc[(j, *here)] = real.astype(jnp.bfloat16)
            acc[(j, *there)] = cross.astype(jnp.bfloat16)

    for x in range(2):
        for lane in range(0, width, LANES):
            products(x, 0, lane, True)

            @pl.loop(1, seg // tile, unroll=seg // tile - 1)
            def _(t):
                products(x, pl.multiple_of(t * tile, tile), lane, False)

        for j in range(segs):
            value = jnp.dot(back[...], acc[j], preferred_element_type=jnp.float32).astype(jnp.bfloat16)
            for core in range(2):
                result[2 * j + core, x] = value[core * rows : (core + 1) * rows]
    me = 2 * spot.chip + spot.core
    for k in range(n):
        outs[k][...] = result[me ^ k]


def correlate(forward, back, kern, pieces):
    ks, flat = tuple(pieces), tuple(pieces.values())
    segs = len(flat)
    _, rows, width = flat[0].shape
    seg = 2 * rows
    n = 2 * segs
    out = array((2, rows, width))
    return call(
        functools.partial(correlate_kernel, ks),
        (forward, back, kern, *flat),
        [whole(forward), whole(back), VMEM] + [whole(p) for p in flat],
        [out] * n,
        [whole(out)] * n,
        "correlate",
        [
            pltpu.VMEM((segs, seg, width), jnp.bfloat16),
            pltpu.VMEM((segs, 2 * seg, width), jnp.float32),
            pltpu.VMEM((segs, 2 * seg, width), jnp.bfloat16),
            pltpu.VMEM((n, *out.shape), jnp.bfloat16),
        ],
    )


def finish_kernel(ks, factor, fetch_branches, spot, *refs):
    n = len(ks)
    if fetch_branches:
        (key, value, *pieces), refs = refs[: 2 + n], refs[2 + n :]
        branches, *outs, key_o, value_o, filter_o, in_sem, out_sem = refs
    else:
        (branches, *pieces), refs = refs[: 1 + n], refs[1 + n :]
        *outs, key_o, value_o, filter_o, in_sem, out_sem = refs
    width = pieces[0].shape[2]
    me = 2 * spot.chip + spot.core
    loads = []
    if fetch_branches:
        loads.append(pltpu.make_async_copy(key, branches.at[0], in_sem.at[n]))
        loads.append(pltpu.make_async_copy(value, branches.at[1], in_sem.at[n + 1]))
    for copy in loads:
        copy.start()
    for copy in loads:
        copy.wait()
    stores = []
    for i, k in enumerate(ks):
        here = (slice(None), pl.ds(pl.multiple_of((me ^ k) * width, width), width))
        conv_grad = pieces[i][0].astype(jnp.float32)
        key_o[i] = (conv_grad * branches[(1, *here)].astype(jnp.float32)).astype(jnp.bfloat16)
        value_o[i] = (conv_grad * branches[(0, *here)].astype(jnp.float32)).astype(jnp.bfloat16)
        filter_o[i] = pieces[i][1].astype(jnp.float32) * factor
        for o, (src, dst) in enumerate(zip((key_o, value_o, filter_o), outs)):
            stores.append(pltpu.make_async_copy(src.at[i], dst.at[here], out_sem.at[o, i]))
            stores[-1].start()
    for copy in stores:
        copy.wait()


def finish(ks, pieces, factor, key=None, value=None, branches=None, grads=None):
    begin = branches is None
    n = len(ks)
    rows, width = pieces[0].shape[1:]
    scratch = [
        pltpu.VMEM((n, rows, width), jnp.bfloat16),
        pltpu.VMEM((n, rows, width), jnp.bfloat16),
        pltpu.VMEM((n, rows, width), jnp.float32),
        pltpu.SemaphoreType.DMA((n + 2,)),
        pltpu.SemaphoreType.DMA((3, n)),
    ]
    kernel = functools.partial(finish_kernel, ks, factor, begin)
    if begin:
        both = pltpu.VMEM((2, *key.shape), key.dtype)
        outs = [both, array(key.shape), array(key.shape), array(key.shape, jnp.float32)]
        args = (key, value, *pieces)
        return call(kernel, args, [ANY, ANY, *[VMEM] * n], outs, [VMEM, *[ANY] * 3], "finish", scratch)
    args = (branches, *pieces)
    return call(kernel, args, [VMEM] * (1 + n), [], [], "finish", scratch, update=grads)


def hold(arrays, after):
    return call(lambda spot: None, (), [], [], [], "hold", carry=arrays, after=after)


def swap(x, k, n):
    return lax.ppermute(x, "seq", [(i, i ^ k) for i in range(n)]) if k else x


def fast_shards(grad_out, out_weight, query_gate, key_branch, value_branch, filter_taps):
    n = lax.axis_size("seq")
    planes = lax.axis_size("ch")
    rows = grad_out.shape[0]
    chips = n // 2
    factor = 1.0 / math.sqrt(rows * n)
    forward, back = (jnp.asarray(t) for t in half_tables(2 * rows))
    outer = [(i, i ^ 1) for i in range(planes)]
    inner = []
    for s in range(n):
        inner += [(s * planes + 1, s * planes + 2), (s * planes + 2, s * planes + 1)]
        inner += [(s * planes + z, (s ^ 1) * planes + z) for z in (0, planes - 1)]

    def send_outer(x):
        return lax.ppermute(x, "ch", outer)

    def send_inner(x):
        return lax.ppermute(x, ("seq", "ch"), inner)

    def other(x):
        return swap(x, 1, n)

    outer_0, inner_0, others = send_outer(grad_out), send_inner(grad_out), other(grad_out)
    mine, *packed, packed_mark = pack(query_gate, key_branch, value_branch, filter_taps, chips)
    gates, taps_input, (merged,) = merge(mine, [other(x) for x in packed], after=[packed_mark])
    taps_input = [swap(x, 2 * k, n) for k, x in enumerate(taps_input)]
    outer_1, inner_1 = send_outer(inner_0), send_inner(outer_0)
    held, loaded = load(out_weight, chips, after=[merged])
    total, first = mix(0, [[grad_out], [others]], held, None, after=[loaded])
    kern, tapped = tap_kernels(forward, taps_input, after=[first])
    outer_1, inner_1, gone = hold([outer_1, inner_1], after=[tapped])
    outer_2 = send_outer(inner_1)
    total, outer_1, second = mix(1, [[outer_0], [other(outer_0)]], held, total, carry=[outer_1], after=[gone])
    blocks = [[outer_1, inner_0], [other(outer_1), other(inner_0)]]
    total, _ = mix(2, blocks, held, total, after=[second])
    gated = mix_gate([[outer_2, inner_1], [other(outer_2), other(inner_1)]], held, total, gates)[:chips]
    order = [0, *sorted(range(1, chips), key=lambda k: (-k.bit_count(), -k))]
    gated = {k: swap(gated[k], 2 * k, n) for k in order}

    results = correlate(forward, back, kern, gated)[:n]
    order = sorted(range(n), key=lambda k: ((k // 2).bit_count(), k % 2, k))
    results = {k: swap(results[k], k, n) for k in order}
    near, far = order[: n // 2], order[n // 2 :]
    branches, *grads, _ = finish(near, [results[k] for k in near], factor, key=key_branch, value=value_branch)
    return tuple(finish(far, [results[k] for k in far], factor, branches=branches, grads=grads)[:3])


def solution(mesh):
    specs = dict(
        mesh=mesh,
        in_specs=(
            P("seq", "ch"),
            P("ch", None),
            P("seq", "ch"),
            P("seq", "ch"),
            P("seq", "ch"),
            P("seq", "ch"),
        ),
        out_specs=(P("seq", "ch"), P("seq", "ch"), P("seq", "ch")),
        check_vma=False,
    )
    n, planes = mesh.shape["seq"], mesh.shape["ch"]

    def step(*arrays):
        whole_tiles = arrays[1].shape[0] // planes % (n * LANES) == 0
        fits = whole_tiles and planes == 4 and n & (n - 1) == 0
        return jax.shard_map(fast_shards if fits else shards, **specs)(*arrays)

    return step
```

```python
import functools
import math

import jax
import jax.numpy as jnp
import ml_dtypes
import numpy as np
from jax import lax
from jax.experimental import pallas as pl
from jax.experimental.pallas import tpu as pltpu
from jax.sharding import PartitionSpec as P

LANES = 128


def build_tables(seg_len):
    twice_length = 2 * seg_len
    freq_index = jnp.arange(twice_length, dtype=jnp.int32)
    row_index = jnp.arange(seg_len, dtype=jnp.int32)
    angle_unit = 2.0 * math.pi / twice_length
    fwd_phase = (freq_index[:, None] * row_index[None, :] % twice_length).astype(
        jnp.float32
    ) * angle_unit
    back_phase = (freq_index[None, :] * (seg_len - row_index[:, None]) % twice_length).astype(
        jnp.float32
    ) * angle_unit
    window_pos = (freq_index + seg_len) % twice_length
    window_phase = (freq_index[None, :] * window_pos[:, None] % twice_length).astype(
        jnp.float32
    ) * angle_unit
    parity = jnp.where(freq_index % 2 == 0, 1.0, -1.0).astype(jnp.float32)[:, None]
    return (
        jnp.cos(fwd_phase).astype(jnp.bfloat16),
        jnp.sin(fwd_phase).astype(jnp.bfloat16),
        jnp.cos(back_phase).astype(jnp.bfloat16),
        jnp.sin(back_phase).astype(jnp.bfloat16),
        jnp.cos(window_phase).astype(jnp.bfloat16),
        jnp.sin(window_phase).astype(jnp.bfloat16),
        parity,
    )


def spectra(block_list, cosine_forward, sine_forward):
    cosine_piece = jnp.einsum(
        "qk,rkb->rqb", cosine_forward, block_list, preferred_element_type=jnp.float32
    )
    sine_piece = jnp.einsum(
        "qk,rkb->rqb", sine_forward, block_list, preferred_element_type=jnp.float32
    )
    return (cosine_piece, sine_piece)


def shards(grad_out, out_weight, query_gate, key_branch, value_branch, filter_taps):
    seg_len = query_gate.shape[0]
    channels = query_gate.shape[1]
    twice_length = 2 * seg_len
    segments = lax.axis_size("seq")
    my_index = lax.axis_index("seq")
    factor = 1.0 / math.sqrt(seg_len * segments)
    grad_mix = lax.dot_general(
        lax.all_gather(grad_out, "ch", axis=1, tiled=True),
        out_weight,
        (((1,), (1,)), ((), ())),
        preferred_element_type=jnp.float32,
    )
    gated_grad = (grad_mix * query_gate.astype(jnp.float32)).astype(jnp.bfloat16)
    conv_input = (key_branch.astype(jnp.float32) * value_branch.astype(jnp.float32)).astype(
        jnp.bfloat16
    )
    tables = build_tables(seg_len)
    (
        cosine_forward,
        sine_forward,
        cosine_backward,
        sine_backward,
        cosine_window,
        sine_window,
        parity,
    ) = tables
    all_taps = lax.all_gather(filter_taps, "seq", axis=0, tiled=True)
    tap_cos, tap_sin = spectra(
        all_taps.reshape(segments, seg_len, channels), cosine_forward, sine_forward
    )
    kern_cos = jnp.concatenate([jnp.zeros_like(tap_cos[:1]), tap_cos[:-1]], 0) + parity * tap_cos
    kern_sin = jnp.concatenate([jnp.zeros_like(tap_sin[:1]), tap_sin[:-1]], 0) + parity * tap_sin
    own_cos, own_sin = spectra(conv_input[None], cosine_forward, sine_forward)
    own_cos = own_cos[0]
    own_sin = own_sin[0]
    zero_spec = jnp.zeros((twice_length, channels), jnp.float32)
    initial = (zero_spec, zero_spec, jnp.zeros(((segments + 1) * seg_len, channels), jnp.float32))
    piece_data = lax.all_gather(gated_grad, "seq", axis=0, tiled=True)
    block_count = piece_data.shape[0] // seg_len
    seg_ids = jnp.arange(block_count, dtype=jnp.int32)
    block_list = piece_data.reshape(block_count, seg_len, channels)
    grad_cos, grad_sin = spectra(block_list, cosine_forward, sine_forward)
    lag_steps = seg_ids - my_index
    inside = seg_ids < segments
    live_mask = ((lag_steps >= 0) & inside).astype(jnp.float32)[:, None, None]
    lag_clip = jnp.clip(lag_steps, 0, segments - 1)
    lag_kcos = jnp.take(kern_cos, lag_clip, axis=0)
    lag_ksin = jnp.take(kern_sin, lag_clip, axis=0)
    running_real = jnp.sum(live_mask * (grad_cos * lag_kcos + grad_sin * lag_ksin), axis=0)
    running_imaginary = jnp.sum(live_mask * (grad_sin * lag_kcos - grad_cos * lag_ksin), axis=0)
    product_real = (own_cos * grad_cos + own_sin * grad_sin).astype(jnp.bfloat16)
    product_imaginary = (own_sin * grad_cos - own_cos * grad_sin).astype(jnp.bfloat16)
    windows = jnp.einsum(
        "an,hny->hay", cosine_window, product_real, preferred_element_type=jnp.float32
    ) - jnp.einsum(
        "an,hny->hay", sine_window, product_imaginary, preferred_element_type=jnp.float32
    )
    windows = windows * (live_mask / twice_length)

    def place(item_index, buffer):
        offset = lag_clip[item_index] * seg_len
        current = lax.dynamic_slice_in_dim(buffer, offset, twice_length, 0)
        return lax.dynamic_update_slice_in_dim(buffer, current + windows[item_index], offset, 0)

    buffer = lax.fori_loop(0, block_list.shape[0], place, initial[2])
    convolution_gradient = (
        jnp.dot(
            cosine_backward, running_real.astype(jnp.bfloat16), preferred_element_type=jnp.float32
        )
        - jnp.dot(
            sine_backward,
            running_imaginary.astype(jnp.bfloat16),
            preferred_element_type=jnp.float32,
        )
    ) / twice_length
    own_rows = lax.psum_scatter(
        buffer[seg_len:].astype(jnp.bfloat16), "seq", scatter_dimension=0, tiled=True
    ).astype(jnp.float32)
    filter_grad = own_rows * factor
    key_grad = (convolution_gradient * value_branch.astype(jnp.float32)).astype(jnp.bfloat16)
    value_grad = (convolution_gradient * key_branch.astype(jnp.float32)).astype(jnp.bfloat16)
    return (key_grad, value_grad, filter_grad)


def half_tables(rows):
    size = 2 * rows
    freq = np.arange(rows)
    pos = np.arange(rows)
    angle = 2.0 * np.pi * (np.outer(freq, pos) % size) / size
    sine = np.sin(angle)
    sine[0] = (-1.0) ** pos
    forward = np.concatenate([np.cos(angle), sine], 0)
    angle = 2.0 * np.pi * (np.outer(rows - pos, freq) % size) / size
    cos_back = 2.0 * np.cos(angle)
    sin_back = -2.0 * np.sin(angle)
    cos_back[:, 0] = 1.0
    sin_back[:, 0] = (-1.0) ** (rows - pos)
    back = np.concatenate([cos_back, sin_back], 1) / size
    return forward.astype(ml_dtypes.bfloat16), back.astype(ml_dtypes.bfloat16)


ANY = pl.BlockSpec(memory_space=pl.ANY)
VMEM = pl.BlockSpec(memory_space=pltpu.VMEM)
MARK = jax.ShapeDtypeStruct((8, LANES), jnp.float32)


class Spot:
    def __init__(self):
        me, plane, planes = lax.axis_index("seq"), lax.axis_index("ch"), lax.axis_size("ch")
        low = plane < planes // 2
        self.chip, self.core = me // 2, me % 2
        self.outer = (plane == 0) | (plane == planes - 1)
        self.blocks = (plane, plane ^ 1, jnp.where(low, 2, 1), jnp.where(low, 3, 0))


def call(kernel, args, in_specs, outs, out_specs, name, scratch=(), limit=24, flops=0, update=(), carry=(), after=()):
    same = (*update, *carry)
    count, results, written = len(args), len(outs), len(outs) + len(update)

    def body(*refs):
        rest = refs[count + len(same) + len(after) :]
        mark, *scratch_refs = rest[results + len(same) :]
        mark[...] = jnp.zeros_like(mark)
        kernel(Spot(), *refs[:count], *rest[:written], *scratch_refs)

    return pl.pallas_call(
        body,
        input_output_aliases={count + i: results + i for i in range(len(same))},
        grid=(1,),
        in_specs=[*in_specs, *[ANY] * (len(same) + len(after))],
        out_specs=[*out_specs, *[ANY] * len(same), whole(MARK)],
        scratch_shapes=scratch,
        out_shape=[*outs, *[array(x.shape, x.dtype) for x in same], MARK],
        compiler_params=pltpu.CompilerParams(vmem_limit_bytes=limit * 2**20),
        cost_estimate=pl.CostEstimate(flops=flops, bytes_accessed=0, transcendentals=0),
        name=name,
    )(*args, *same, *after)


def whole(x):
    return pl.BlockSpec(x.shape, lambda *_: (0,) * len(x.shape))


def array(shape, dtype=jnp.bfloat16):
    return jax.ShapeDtypeStruct(shape, dtype)


def place(spot, k, core, width):
    return pl.multiple_of(((spot.chip ^ k) * 2 + core) * width, width)


def load_kernel(chips, spot, weight, held, sem):
    width = held.shape[1]
    depth = held.shape[2] // 4
    copies = []
    for b in range(4):
        at = pl.multiple_of(spot.blocks[b] * depth, depth)
        for k in range(chips):
            rows = pl.ds(place(spot, k, spot.core, width), width)
            copies.append(
                pltpu.make_async_copy(
                    weight.at[rows, pl.ds(at, depth)],
                    held.at[k, :, pl.ds(b * depth, depth)],
                    sem.at[b * chips + k],
                )
            )
    for copy in copies:
        copy.start()
    for copy in copies:
        copy.wait()


def load(weight, chips, **order):
    held = (chips, weight.shape[0] // (2 * chips), weight.shape[1])
    return call(
        functools.partial(load_kernel, chips),
        (weight,),
        [ANY],
        [pltpu.VMEM(held, weight.dtype)],
        [VMEM],
        "load_weight",
        [pltpu.SemaphoreType.DMA((4 * chips,))],
        **order,
    )


def pack_kernel(chips, spot, gate, key, value, taps, mine, theirs_0, theirs_1, all_in, sem):
    width = mine.shape[3]
    half = theirs_0.shape[2]
    loads = [pltpu.make_async_copy(ref, all_in.at[i], sem.at[i]) for i, ref in enumerate((gate, taps, key, value))]
    for copy in loads:
        copy.start()
    for copy in loads:
        copy.wait()
    upper, lower = slice(0, half), slice(half, 2 * half)
    for out, core, rows in (
        (theirs_0, 1 - spot.core, upper),
        (theirs_1, 1 - spot.core, lower),
        (mine, spot.core, slice(None)),
    ):
        for k in range(chips):
            here = (rows, pl.ds(place(spot, k, core, width), width))
            out[0, k] = all_in[(0, *here)]
            out[1, k] = all_in[(1, *here)]
            product = all_in[(2, *here)].astype(jnp.float32) * all_in[(3, *here)].astype(jnp.float32)
            out[2, k] = product.astype(jnp.bfloat16)


def pack(gate, key, value, taps, chips, **order):
    rows, channels = key.shape
    out = (3, chips, rows, channels // (2 * chips))
    half = array((3, chips, rows // 2, channels // (2 * chips)))
    return call(
        functools.partial(pack_kernel, chips),
        (gate, key, value, taps),
        [ANY] * 4,
        [pltpu.VMEM(out, jnp.bfloat16), half, half],
        [VMEM, whole(half), whole(half)],
        "pack_core",
        [pltpu.VMEM((4, rows, channels), jnp.bfloat16), pltpu.SemaphoreType.DMA((4,))],
        limit=58,
        **order,
    )


def merge_kernel(spot, mine, other_0, other_1, gates, *refs):
    *outs, sem = refs
    own, theirs = spot.core, 1 - spot.core
    half = other_0.shape[2]
    loads = []
    for h, other in enumerate((other_0, other_1)):
        rows = pl.ds(h * half, half)
        for k, out in enumerate(outs):
            for i, to in enumerate((gates.at[k, 1, rows], out.at[0, theirs, rows], out.at[1, theirs, rows])):
                loads.append(pltpu.make_async_copy(other.at[i, k], to, sem.at[len(loads)]))
    for copy in loads:
        copy.start()
    for k, out in enumerate(outs):
        gates[k, 0] = mine[0, k]
        out[0, own] = mine[1, k]
        out[1, own] = mine[2, k]
    for copy in loads:
        copy.wait()


def merge(mine, others, **order):
    _, chips, rows, width = mine.shape
    piece = array((2, 2, rows, width))
    out = call(
        merge_kernel,
        (mine, *others),
        [VMEM, ANY, ANY],
        [pltpu.VMEM((chips, 2, rows, width), jnp.bfloat16)] + [piece] * chips,
        [VMEM] + [whole(piece)] * chips,
        "merge_cores",
        [pltpu.SemaphoreType.DMA((6 * chips,))],
        **order,
    )
    return out[0], out[1 : 1 + chips], out[1 + chips :]


def contract(x, w):
    return lax.dot_general(x, w, (((1,), (1,)), ((), ())), preferred_element_type=jnp.float32)


def fetch(spot, groups, x, sem):
    rows = groups[0][0].shape[0]
    for i, group in enumerate(groups):
        to = x.at[pl.ds(i * rows, rows)]
        for j, ref in enumerate(group):
            copy = pltpu.make_async_copy(ref, to, sem.at[i])
            if len(group) == 1:
                copy.start()
            else:
                pl.when(spot.outer if j == 0 else ~spot.outer)(copy.start)
    for i, group in enumerate(groups):
        pltpu.make_async_copy(group[0], x.at[pl.ds(i * rows, rows)], sem.at[i]).wait()


def grouped(refs, sizes):
    refs = list(refs)
    return [[refs.pop(0) for _ in range(s)] for s in sizes]


def mix_kernel(block, sizes, has_total, spot, *refs):
    count = sum(sizes)
    groups = grouped(refs[:count], sizes)
    held, *rest = refs[count:]
    total, out, x, sem = rest if has_total else (None, *rest)
    depth = x.shape[1]
    fetch(spot, groups, x, sem)

    @pl.loop(0, held.shape[0])
    def _(k):
        value = contract(x[...], held[k, :, block * depth : (block + 1) * depth])
        out[k] = value + total[k] if has_total else value


def mix(block, groups, held, total, **order):
    chips, width, _ = held.shape
    sizes = [len(g) for g in groups]
    flat = [x for g in groups for x in g]
    rows = sum(g[0].shape[0] for g in groups)
    depth = flat[0].shape[1]
    out = (chips, rows, width)
    return call(
        functools.partial(mix_kernel, block, sizes, total is not None),
        (*flat, held) + ((total,) if total is not None else ()),
        [ANY] * len(flat) + [VMEM] + ([VMEM] if total is not None else []),
        [pltpu.VMEM(out, jnp.float32)],
        [VMEM],
        "mix",
        [pltpu.VMEM((rows, depth), jnp.bfloat16), pltpu.SemaphoreType.DMA((len(groups),))],
        **order,
    )


def gate_kernel(sizes, spot, *refs):
    count = sum(sizes)
    groups = grouped(refs[:count], sizes)
    held, total, gates, *outs, x, sem = refs[count:]
    depth = x.shape[1]
    rows = x.shape[0] // 2
    fetch(spot, groups, x, sem)
    for k, out in enumerate(outs):
        value = contract(x[...], held[k, :, 3 * depth : 4 * depth])
        for h, core in enumerate((spot.core, 1 - spot.core)):
            own = slice(h * rows, (h + 1) * rows)
            mixed = total[k, own] + value[own]
            out[core] = (mixed * gates[k, h].astype(jnp.float32)).astype(jnp.bfloat16)


def mix_gate(groups, held, total, gates):
    chips, width, _ = held.shape
    sizes = [len(g) for g in groups]
    flat = [x for g in groups for x in g]
    rows, depth = flat[0].shape
    piece = array((2, rows, width))
    return call(
        functools.partial(gate_kernel, sizes),
        (*flat, held, total, gates),
        [ANY] * len(flat) + [VMEM] * 3,
        [piece] * chips,
        [whole(piece)] * chips,
        "mix_gate",
        [pltpu.VMEM((2 * rows, depth), jnp.bfloat16), pltpu.SemaphoreType.DMA((len(groups),))],
    )


def tap_kernel(spot, forward, *refs):
    *pieces, out, spec = refs
    segs = len(pieces)
    seg = forward.shape[1]
    width = pieces[0].shape[3]
    row = lax.broadcasted_iota(jnp.int32, (2 * seg, width), 0)
    sign = jnp.where(row % 2 == 0, 1.0, -1.0)
    for x in range(2):
        for k, piece in enumerate(pieces):
            block = piece[x].reshape(seg, width)
            spec[spot.chip ^ k] = jnp.dot(forward[...], block, preferred_element_type=jnp.float32)
        for r in range(segs):
            kern = sign * spec[r]
            if r:
                kern += spec[r - 1]
            out[x, r] = kern.astype(jnp.bfloat16)


def tap_kernels(forward, pieces, **order):
    segs = len(pieces)
    width = pieces[0].shape[3]
    shape = (2, segs, *forward.shape[:1], width)
    return call(
        tap_kernel,
        (forward, *pieces),
        [whole(forward)] + [whole(p) for p in pieces],
        [pltpu.VMEM(shape, jnp.bfloat16)],
        [VMEM],
        "kernels",
        [pltpu.VMEM(shape[1:], jnp.float32)],
        flops=12 * math.prod(shape) * forward.shape[1],
        **order,
    )


def correlate_kernel(ks, spot, forward, back, kern, *refs):
    segs = kern.shape[1]
    n = 2 * segs
    pieces = refs[:segs]
    outs = refs[segs : segs + n]
    data, spec, acc, result = refs[segs + n :]
    rows = pieces[0].shape[1]
    seg = 2 * rows
    width = data.shape[2]
    for k, piece in zip(ks, pieces):
        for core in range(2):
            data[spot.chip ^ k, core * rows : (core + 1) * rows] = piece[core]
    for i in range(segs):
        spec[i] = jnp.dot(forward[...], data[i], preferred_element_type=jnp.float32)

    tile = 16

    def products(x, row, lane, first):
        here = (pl.ds(row, tile), pl.ds(lane, LANES))
        there = (pl.ds(row + seg, tile), pl.ds(lane, LANES))
        g_real = [spec[(i, *here)] for i in range(segs)]
        g_imag = [spec[(i, *there)] for i in range(segs)]
        k_real = [kern[(x, r, *here)].astype(jnp.float32) for r in range(segs)]
        k_imag = [kern[(x, r, *there)].astype(jnp.float32) for r in range(segs)]
        if first:
            edge = lax.broadcasted_iota(jnp.int32, (tile, LANES), 0) == 0
        for j in range(segs):
            both = sum(g_real[i] * k_real[i - j] for i in range(j, segs))
            other = sum(g_imag[i] * k_imag[i - j] for i in range(j, segs))
            cross = sum(g_imag[i] * k_real[i - j] - g_real[i] * k_imag[i - j] for i in range(j, segs))
            if first:
                real = both + jnp.where(edge, 0.0, other)
                cross = jnp.where(edge, other, cross)
            else:
                real = both + other
            acc[(j, *here)] = real.astype(jnp.bfloat16)
            acc[(j, *there)] = cross.astype(jnp.bfloat16)

    for x in range(2):
        for lane in range(0, width, LANES):
            products(x, 0, lane, True)

            @pl.loop(1, seg // tile, unroll=seg // tile - 1)
            def _(t):
                products(x, pl.multiple_of(t * tile, tile), lane, False)

        for j in range(segs):
            value = jnp.dot(back[...], acc[j], preferred_element_type=jnp.float32).astype(jnp.bfloat16)
            for core in range(2):
                result[2 * j + core, x] = value[core * rows : (core + 1) * rows]
    me = 2 * spot.chip + spot.core
    for k in range(n):
        outs[k][...] = result[me ^ k]


def correlate(forward, back, kern, pieces):
    ks, flat = tuple(pieces), tuple(pieces.values())
    segs = len(flat)
    _, rows, width = flat[0].shape
    seg = 2 * rows
    n = 2 * segs
    out = array((2, rows, width))
    return call(
        functools.partial(correlate_kernel, ks),
        (forward, back, kern, *flat),
        [whole(forward), whole(back), VMEM] + [whole(p) for p in flat],
        [out] * n,
        [whole(out)] * n,
        "correlate",
        [
            pltpu.VMEM((segs, seg, width), jnp.bfloat16),
            pltpu.VMEM((segs, 2 * seg, width), jnp.float32),
            pltpu.VMEM((segs, 2 * seg, width), jnp.bfloat16),
            pltpu.VMEM((n, *out.shape), jnp.bfloat16),
        ],
    )


def finish_kernel(ks, factor, fetch_branches, spot, *refs):
    n = len(ks)
    if fetch_branches:
        (key, value, *pieces), refs = refs[: 2 + n], refs[2 + n :]
        branches, *outs, key_o, value_o, filter_o, in_sem, out_sem = refs
    else:
        (branches, *pieces), refs = refs[: 1 + n], refs[1 + n :]
        *outs, key_o, value_o, filter_o, in_sem, out_sem = refs
    width = pieces[0].shape[2]
    me = 2 * spot.chip + spot.core
    loads = []
    if fetch_branches:
        loads.append(pltpu.make_async_copy(key, branches.at[0], in_sem.at[n]))
        loads.append(pltpu.make_async_copy(value, branches.at[1], in_sem.at[n + 1]))
    for copy in loads:
        copy.start()
    for copy in loads:
        copy.wait()
    stores = []
    for i, k in enumerate(ks):
        here = (slice(None), pl.ds(pl.multiple_of((me ^ k) * width, width), width))
        conv_grad = pieces[i][0].astype(jnp.float32)
        key_o[i] = (conv_grad * branches[(1, *here)].astype(jnp.float32)).astype(jnp.bfloat16)
        value_o[i] = (conv_grad * branches[(0, *here)].astype(jnp.float32)).astype(jnp.bfloat16)
        filter_o[i] = pieces[i][1].astype(jnp.float32) * factor
        for o, (src, dst) in enumerate(zip((key_o, value_o, filter_o), outs)):
            stores.append(pltpu.make_async_copy(src.at[i], dst.at[here], out_sem.at[o, i]))
            stores[-1].start()
    for copy in stores:
        copy.wait()


def finish(ks, pieces, factor, key=None, value=None, branches=None, grads=None):
    begin = branches is None
    n = len(ks)
    rows, width = pieces[0].shape[1:]
    scratch = [
        pltpu.VMEM((n, rows, width), jnp.bfloat16),
        pltpu.VMEM((n, rows, width), jnp.bfloat16),
        pltpu.VMEM((n, rows, width), jnp.float32),
        pltpu.SemaphoreType.DMA((n + 2,)),
        pltpu.SemaphoreType.DMA((3, n)),
    ]
    kernel = functools.partial(finish_kernel, ks, factor, begin)
    if begin:
        both = pltpu.VMEM((2, *key.shape), key.dtype)
        outs = [both, array(key.shape), array(key.shape), array(key.shape, jnp.float32)]
        args = (key, value, *pieces)
        return call(kernel, args, [ANY, ANY, *[VMEM] * n], outs, [VMEM, *[ANY] * 3], "finish", scratch)
    args = (branches, *pieces)
    return call(kernel, args, [VMEM] * (1 + n), [], [], "finish", scratch, update=grads)


def hold(arrays, after):
    return call(lambda spot: None, (), [], [], [], "hold", carry=arrays, after=after)


def swap(x, k, n):
    return lax.ppermute(x, "seq", [(i, i ^ k) for i in range(n)]) if k else x


def fast_shards(grad_out, out_weight, query_gate, key_branch, value_branch, filter_taps):
    n = lax.axis_size("seq")
    planes = lax.axis_size("ch")
    rows = grad_out.shape[0]
    chips = n // 2
    factor = 1.0 / math.sqrt(rows * n)
    forward, back = (jnp.asarray(t) for t in half_tables(2 * rows))
    outer = [(i, i ^ 1) for i in range(planes)]
    inner = []
    for s in range(n):
        inner += [(s * planes + 1, s * planes + 2), (s * planes + 2, s * planes + 1)]
        inner += [(s * planes + z, (s ^ 1) * planes + z) for z in (0, planes - 1)]

    def send_outer(x):
        return lax.ppermute(x, "ch", outer)

    def send_inner(x):
        return lax.ppermute(x, ("seq", "ch"), inner)

    def other(x):
        return swap(x, 1, n)

    outer_0, inner_0, others = send_outer(grad_out), send_inner(grad_out), other(grad_out)
    mine, *packed, packed_mark = pack(query_gate, key_branch, value_branch, filter_taps, chips)
    gates, taps_input, (merged,) = merge(mine, [other(x) for x in packed], after=[packed_mark])
    taps_input = [swap(x, 2 * k, n) for k, x in enumerate(taps_input)]
    outer_1, inner_1 = send_outer(inner_0), send_inner(outer_0)
    held, loaded = load(out_weight, chips, after=[merged])
    kern, tapped = tap_kernels(forward, taps_input, after=[loaded])
    outer_1, inner_1, gone = hold([outer_1, inner_1], after=[tapped])
    outer_2 = send_outer(inner_1)
    total, first = mix(0, [[grad_out], [others]], held, None, after=[gone])
    total, outer_1, second = mix(1, [[outer_0], [other(outer_0)]], held, total, carry=[outer_1], after=[first])
    blocks = [[outer_1, inner_0], [other(outer_1), other(inner_0)]]
    total, _ = mix(2, blocks, held, total, after=[second])
    gated = mix_gate([[outer_2, inner_1], [other(outer_2), other(inner_1)]], held, total, gates)[:chips]
    order = [0, *sorted(range(1, chips), key=lambda k: (-k.bit_count(), -k))]
    gated = {k: swap(gated[k], 2 * k, n) for k in order}

    results = correlate(forward, back, kern, gated)[:n]
    order = sorted(range(n), key=lambda k: ((k // 2).bit_count(), k % 2, k))
    results = {k: swap(results[k], k, n) for k in order}
    near, far = order[: n // 2], order[n // 2 :]
    branches, *grads, _ = finish(near, [results[k] for k in near], factor, key=key_branch, value=value_branch)
    return tuple(finish(far, [results[k] for k in far], factor, branches=branches, grads=grads)[:3])


def solution(mesh):
    specs = dict(
        mesh=mesh,
        in_specs=(
            P("seq", "ch"),
            P("ch", None),
            P("seq", "ch"),
            P("seq", "ch"),
            P("seq", "ch"),
            P("seq", "ch"),
        ),
        out_specs=(P("seq", "ch"), P("seq", "ch"), P("seq", "ch")),
        check_vma=False,
    )
    n, planes = mesh.shape["seq"], mesh.shape["ch"]

    def step(*arrays):
        whole_tiles = arrays[1].shape[0] // planes % (n * LANES) == 0
        fits = whole_tiles and planes == 4 and n & (n - 1) == 0
        return jax.shard_map(fast_shards if fits else shards, **specs)(*arrays)

    return step
```

```python
import functools
import math

import jax
import jax.numpy as jnp
import ml_dtypes
import numpy as np
from jax import lax
from jax.experimental import pallas as pl
from jax.experimental.pallas import tpu as pltpu
from jax.sharding import PartitionSpec as P

LANES = 128
PIECES = 4


def build_tables(seg_len):
    twice_length = 2 * seg_len
    freq_index = jnp.arange(twice_length, dtype=jnp.int32)
    row_index = jnp.arange(seg_len, dtype=jnp.int32)
    angle_unit = 2.0 * math.pi / twice_length
    fwd_phase = (freq_index[:, None] * row_index[None, :] % twice_length).astype(
        jnp.float32
    ) * angle_unit
    back_phase = (freq_index[None, :] * (seg_len - row_index[:, None]) % twice_length).astype(
        jnp.float32
    ) * angle_unit
    window_pos = (freq_index + seg_len) % twice_length
    window_phase = (freq_index[None, :] * window_pos[:, None] % twice_length).astype(
        jnp.float32
    ) * angle_unit
    parity = jnp.where(freq_index % 2 == 0, 1.0, -1.0).astype(jnp.float32)[:, None]
    return (
        jnp.cos(fwd_phase).astype(jnp.bfloat16),
        jnp.sin(fwd_phase).astype(jnp.bfloat16),
        jnp.cos(back_phase).astype(jnp.bfloat16),
        jnp.sin(back_phase).astype(jnp.bfloat16),
        jnp.cos(window_phase).astype(jnp.bfloat16),
        jnp.sin(window_phase).astype(jnp.bfloat16),
        parity,
    )


def spectra(block_list, cosine_forward, sine_forward):
    cosine_piece = jnp.einsum(
        "qk,rkb->rqb", cosine_forward, block_list, preferred_element_type=jnp.float32
    )
    sine_piece = jnp.einsum(
        "qk,rkb->rqb", sine_forward, block_list, preferred_element_type=jnp.float32
    )
    return (cosine_piece, sine_piece)


def shards(grad_out, out_weight, query_gate, key_branch, value_branch, filter_taps):
    seg_len = query_gate.shape[0]
    channels = query_gate.shape[1]
    twice_length = 2 * seg_len
    segments = lax.axis_size("seq")
    my_index = lax.axis_index("seq")
    factor = 1.0 / math.sqrt(seg_len * segments)
    grad_mix = lax.dot_general(
        lax.all_gather(grad_out, "ch", axis=1, tiled=True),
        out_weight,
        (((1,), (1,)), ((), ())),
        preferred_element_type=jnp.float32,
    )
    gated_grad = (grad_mix * query_gate.astype(jnp.float32)).astype(jnp.bfloat16)
    conv_input = (key_branch.astype(jnp.float32) * value_branch.astype(jnp.float32)).astype(
        jnp.bfloat16
    )
    tables = build_tables(seg_len)
    (
        cosine_forward,
        sine_forward,
        cosine_backward,
        sine_backward,
        cosine_window,
        sine_window,
        parity,
    ) = tables
    all_taps = lax.all_gather(filter_taps, "seq", axis=0, tiled=True)
    tap_cos, tap_sin = spectra(
        all_taps.reshape(segments, seg_len, channels), cosine_forward, sine_forward
    )
    kern_cos = jnp.concatenate([jnp.zeros_like(tap_cos[:1]), tap_cos[:-1]], 0) + parity * tap_cos
    kern_sin = jnp.concatenate([jnp.zeros_like(tap_sin[:1]), tap_sin[:-1]], 0) + parity * tap_sin
    own_cos, own_sin = spectra(conv_input[None], cosine_forward, sine_forward)
    own_cos = own_cos[0]
    own_sin = own_sin[0]
    zero_spec = jnp.zeros((twice_length, channels), jnp.float32)
    initial = (zero_spec, zero_spec, jnp.zeros(((segments + 1) * seg_len, channels), jnp.float32))
    piece_data = lax.all_gather(gated_grad, "seq", axis=0, tiled=True)
    block_count = piece_data.shape[0] // seg_len
    seg_ids = jnp.arange(block_count, dtype=jnp.int32)
    block_list = piece_data.reshape(block_count, seg_len, channels)
    grad_cos, grad_sin = spectra(block_list, cosine_forward, sine_forward)
    lag_steps = seg_ids - my_index
    inside = seg_ids < segments
    live_mask = ((lag_steps >= 0) & inside).astype(jnp.float32)[:, None, None]
    lag_clip = jnp.clip(lag_steps, 0, segments - 1)
    lag_kcos = jnp.take(kern_cos, lag_clip, axis=0)
    lag_ksin = jnp.take(kern_sin, lag_clip, axis=0)
    running_real = jnp.sum(live_mask * (grad_cos * lag_kcos + grad_sin * lag_ksin), axis=0)
    running_imaginary = jnp.sum(live_mask * (grad_sin * lag_kcos - grad_cos * lag_ksin), axis=0)
    product_real = (own_cos * grad_cos + own_sin * grad_sin).astype(jnp.bfloat16)
    product_imaginary = (own_sin * grad_cos - own_cos * grad_sin).astype(jnp.bfloat16)
    windows = jnp.einsum(
        "an,hny->hay", cosine_window, product_real, preferred_element_type=jnp.float32
    ) - jnp.einsum(
        "an,hny->hay", sine_window, product_imaginary, preferred_element_type=jnp.float32
    )
    windows = windows * (live_mask / twice_length)

    def place(item_index, buffer):
        offset = lag_clip[item_index] * seg_len
        current = lax.dynamic_slice_in_dim(buffer, offset, twice_length, 0)
        return lax.dynamic_update_slice_in_dim(buffer, current + windows[item_index], offset, 0)

    buffer = lax.fori_loop(0, block_list.shape[0], place, initial[2])
    convolution_gradient = (
        jnp.dot(
            cosine_backward, running_real.astype(jnp.bfloat16), preferred_element_type=jnp.float32
        )
        - jnp.dot(
            sine_backward,
            running_imaginary.astype(jnp.bfloat16),
            preferred_element_type=jnp.float32,
        )
    ) / twice_length
    own_rows = lax.psum_scatter(
        buffer[seg_len:].astype(jnp.bfloat16), "seq", scatter_dimension=0, tiled=True
    ).astype(jnp.float32)
    filter_grad = own_rows * factor
    key_grad = (convolution_gradient * value_branch.astype(jnp.float32)).astype(jnp.bfloat16)
    value_grad = (convolution_gradient * key_branch.astype(jnp.float32)).astype(jnp.bfloat16)
    return (key_grad, value_grad, filter_grad)


def half_tables(rows):
    size = 2 * rows
    freq = np.arange(rows)
    pos = np.arange(rows)
    angle = 2.0 * np.pi * (np.outer(freq, pos) % size) / size
    sine = np.sin(angle)
    sine[0] = (-1.0) ** pos
    forward = np.concatenate([np.cos(angle), sine], 0)
    angle = 2.0 * np.pi * (np.outer(rows - pos, freq) % size) / size
    cos_back = 2.0 * np.cos(angle)
    sin_back = -2.0 * np.sin(angle)
    cos_back[:, 0] = 1.0
    sin_back[:, 0] = (-1.0) ** (rows - pos)
    back = np.concatenate([cos_back, sin_back], 1) / size
    return forward.astype(ml_dtypes.bfloat16), back.astype(ml_dtypes.bfloat16)


ANY = pl.BlockSpec(memory_space=pl.ANY)
VMEM = pl.BlockSpec(memory_space=pltpu.VMEM)
MARK = jax.ShapeDtypeStruct((8, LANES), jnp.float32)


class Spot:
    def __init__(self):
        me, plane, planes = lax.axis_index("seq"), lax.axis_index("ch"), lax.axis_size("ch")
        low = plane < planes // 2
        self.chip, self.core = me // 2, me % 2
        self.outer = (plane == 0) | (plane == planes - 1)
        self.blocks = (plane, plane ^ 1, jnp.where(low, 2, 1), jnp.where(low, 3, 0))


def call(kernel, args, in_specs, outs, out_specs, name, scratch=(), limit=24, flops=0, update=(), carry=(), after=()):
    same = (*update, *carry)
    count, results, written = len(args), len(outs), len(outs) + len(update)

    def body(*refs):
        rest = refs[count + len(same) + len(after) :]
        mark, *scratch_refs = rest[results + len(same) :]
        mark[...] = jnp.zeros_like(mark)
        kernel(Spot(), *refs[:count], *rest[:written], *scratch_refs)

    return pl.pallas_call(
        body,
        input_output_aliases={count + i: results + i for i in range(len(same))},
        grid=(1,),
        in_specs=[*in_specs, *[ANY] * (len(same) + len(after))],
        out_specs=[*out_specs, *[ANY] * len(same), whole(MARK)],
        scratch_shapes=scratch,
        out_shape=[*outs, *[array(x.shape, x.dtype) for x in same], MARK],
        compiler_params=pltpu.CompilerParams(vmem_limit_bytes=limit * 2**20),
        cost_estimate=pl.CostEstimate(flops=flops, bytes_accessed=0, transcendentals=0),
        name=name,
    )(*args, *same, *after)


def whole(x):
    return pl.BlockSpec(x.shape, lambda *_: (0,) * len(x.shape))


def array(shape, dtype=jnp.bfloat16):
    return jax.ShapeDtypeStruct(shape, dtype)


def place(spot, k, core, width):
    return pl.multiple_of(((spot.chip ^ k) * 2 + core) * width, width)


def load_kernel(chips, spot, weight, held, sem):
    width = held.shape[1]
    depth = held.shape[2] // 4
    copies = []
    for b in range(4):
        at = pl.multiple_of(spot.blocks[b] * depth, depth)
        for k in range(chips):
            rows = pl.ds(place(spot, k, spot.core, width), width)
            copies.append(
                pltpu.make_async_copy(
                    weight.at[rows, pl.ds(at, depth)],
                    held.at[k, :, pl.ds(b * depth, depth)],
                    sem.at[b * chips + k],
                )
            )
    for copy in copies:
        copy.start()
    for copy in copies:
        copy.wait()


def load(weight, chips, **order):
    held = (chips, weight.shape[0] // (2 * chips), weight.shape[1])
    return call(
        functools.partial(load_kernel, chips),
        (weight,),
        [ANY],
        [pltpu.VMEM(held, weight.dtype)],
        [VMEM],
        "load_weight",
        [pltpu.SemaphoreType.DMA((4 * chips,))],
        **order,
    )


def pack_kernel(chips, spot, gate, key, value, taps, mine, theirs_0, theirs_1, all_in, sem):
    width = mine.shape[3]
    half = theirs_0.shape[2]
    loads = [pltpu.make_async_copy(ref, all_in.at[i], sem.at[i]) for i, ref in enumerate((gate, taps, key, value))]
    for copy in loads:
        copy.start()
    for copy in loads:
        copy.wait()
    upper, lower = slice(0, half), slice(half, 2 * half)
    for out, core, rows in (
        (theirs_0, 1 - spot.core, upper),
        (theirs_1, 1 - spot.core, lower),
        (mine, spot.core, slice(None)),
    ):
        for k in range(chips):
            here = (rows, pl.ds(place(spot, k, core, width), width))
            out[0, k] = all_in[(0, *here)]
            out[1, k] = all_in[(1, *here)]
            product = all_in[(2, *here)].astype(jnp.float32) * all_in[(3, *here)].astype(jnp.float32)
            out[2, k] = product.astype(jnp.bfloat16)


def pack(gate, key, value, taps, chips, **order):
    rows, channels = key.shape
    out = (3, chips, rows, channels // (2 * chips))
    half = array((3, chips, rows // 2, channels // (2 * chips)))
    return call(
        functools.partial(pack_kernel, chips),
        (gate, key, value, taps),
        [ANY] * 4,
        [pltpu.VMEM(out, jnp.bfloat16), half, half],
        [VMEM, whole(half), whole(half)],
        "pack_core",
        [pltpu.VMEM((4, rows, channels), jnp.bfloat16), pltpu.SemaphoreType.DMA((4,))],
        limit=58,
        **order,
    )


def merge_kernel(spot, mine, other_0, other_1, gates, *refs):
    *outs, sem = refs
    own, theirs = spot.core, 1 - spot.core
    half = other_0.shape[2]
    loads = []
    for h, other in enumerate((other_0, other_1)):
        rows = pl.ds(h * half, half)
        for k, out in enumerate(outs):
            for i, to in enumerate((gates.at[k, 1, rows], out.at[0, theirs, rows], out.at[1, theirs, rows])):
                loads.append(pltpu.make_async_copy(other.at[i, k], to, sem.at[len(loads)]))
    for copy in loads:
        copy.start()
    for k, out in enumerate(outs):
        gates[k, 0] = mine[0, k]
        out[0, own] = mine[1, k]
        out[1, own] = mine[2, k]
    for copy in loads:
        copy.wait()


def merge(mine, others, **order):
    _, chips, rows, width = mine.shape
    piece = array((2, 2, rows, width))
    out = call(
        merge_kernel,
        (mine, *others),
        [VMEM, ANY, ANY],
        [pltpu.VMEM((chips, 2, rows, width), jnp.bfloat16)] + [piece] * chips,
        [VMEM] + [whole(piece)] * chips,
        "merge_cores",
        [pltpu.SemaphoreType.DMA((6 * chips,))],
        **order,
    )
    return out[0], out[1 : 1 + chips], out[1 + chips :]


def contract(x, w):
    return lax.dot_general(x, w, (((1,), (1,)), ((), ())), preferred_element_type=jnp.float32)


def fetch(spot, groups, x, sem):
    rows = groups[0][0].shape[0] // PIECES
    waits = []
    for i, group in enumerate(groups):
        for p in range(PIECES):
            at = i * PIECES + p
            to = x.at[pl.ds(at * rows, rows)]
            copies = [pltpu.make_async_copy(ref.at[pl.ds(p * rows, rows)], to, sem.at[at]) for ref in group]
            if len(group) == 1:
                copies[0].start()
            else:
                pl.when(spot.outer)(copies[0].start)
                pl.when(~spot.outer)(copies[1].start)
            waits.append(copies[0])
    for copy in waits:
        copy.wait()


def grouped(refs, sizes):
    refs = list(refs)
    return [[refs.pop(0) for _ in range(s)] for s in sizes]


def mix_kernel(block, sizes, has_total, spot, *refs):
    count = sum(sizes)
    groups = grouped(refs[:count], sizes)
    held, *rest = refs[count:]
    total, out, x, sem = rest if has_total else (None, *rest)
    depth = x.shape[1]
    fetch(spot, groups, x, sem)

    @pl.loop(0, held.shape[0])
    def _(k):
        value = contract(x[...], held[k, :, block * depth : (block + 1) * depth])
        out[k] = value + total[k] if has_total else value


def mix(block, groups, held, total, **order):
    chips, width, _ = held.shape
    sizes = [len(g) for g in groups]
    flat = [x for g in groups for x in g]
    rows = sum(g[0].shape[0] for g in groups)
    depth = flat[0].shape[1]
    out = (chips, rows, width)
    return call(
        functools.partial(mix_kernel, block, sizes, total is not None),
        (*flat, held) + ((total,) if total is not None else ()),
        [ANY] * len(flat) + [VMEM] + ([VMEM] if total is not None else []),
        [pltpu.VMEM(out, jnp.float32)],
        [VMEM],
        "mix",
        [pltpu.VMEM((rows, depth), jnp.bfloat16), pltpu.SemaphoreType.DMA((PIECES * len(groups),))],
        **order,
    )


def gate_kernel(sizes, spot, *refs):
    count = sum(sizes)
    groups = grouped(refs[:count], sizes)
    held, total, gates, *outs, x, sem = refs[count:]
    depth = x.shape[1]
    rows = x.shape[0] // 2
    fetch(spot, groups, x, sem)
    for k, out in enumerate(outs):
        value = contract(x[...], held[k, :, 3 * depth : 4 * depth])
        for h, core in enumerate((spot.core, 1 - spot.core)):
            own = slice(h * rows, (h + 1) * rows)
            mixed = total[k, own] + value[own]
            out[core] = (mixed * gates[k, h].astype(jnp.float32)).astype(jnp.bfloat16)


def mix_gate(groups, held, total, gates):
    chips, width, _ = held.shape
    sizes = [len(g) for g in groups]
    flat = [x for g in groups for x in g]
    rows, depth = flat[0].shape
    piece = array((2, rows, width))
    return call(
        functools.partial(gate_kernel, sizes),
        (*flat, held, total, gates),
        [ANY] * len(flat) + [VMEM] * 3,
        [piece] * chips,
        [whole(piece)] * chips,
        "mix_gate",
        [pltpu.VMEM((2 * rows, depth), jnp.bfloat16), pltpu.SemaphoreType.DMA((PIECES * len(groups),))],
    )


def tap_kernel(spot, forward, *refs):
    *pieces, out, spec = refs
    segs = len(pieces)
    seg = forward.shape[1]
    width = pieces[0].shape[3]
    row = lax.broadcasted_iota(jnp.int32, (2 * seg, width), 0)
    sign = jnp.where(row % 2 == 0, 1.0, -1.0)
    for x in range(2):
        for k, piece in enumerate(pieces):
            block = piece[x].reshape(seg, width)
            spec[spot.chip ^ k] = jnp.dot(forward[...], block, preferred_element_type=jnp.float32)
        for r in range(segs):
            kern = sign * spec[r]
            if r:
                kern += spec[r - 1]
            out[x, r] = kern.astype(jnp.bfloat16)


def tap_kernels(forward, pieces, **order):
    segs = len(pieces)
    width = pieces[0].shape[3]
    shape = (2, segs, *forward.shape[:1], width)
    return call(
        tap_kernel,
        (forward, *pieces),
        [whole(forward)] + [whole(p) for p in pieces],
        [pltpu.VMEM(shape, jnp.bfloat16)],
        [VMEM],
        "kernels",
        [pltpu.VMEM(shape[1:], jnp.float32)],
        flops=12 * math.prod(shape) * forward.shape[1],
        **order,
    )


def correlate_kernel(ks, spot, forward, back, kern, *refs):
    segs = kern.shape[1]
    n = 2 * segs
    pieces = refs[:segs]
    outs = refs[segs : segs + n]
    data, spec, acc, result = refs[segs + n :]
    rows = pieces[0].shape[1]
    seg = 2 * rows
    width = data.shape[2]
    for k, piece in zip(ks, pieces):
        for core in range(2):
            data[spot.chip ^ k, core * rows : (core + 1) * rows] = piece[core]
    for i in range(segs):
        spec[i] = jnp.dot(forward[...], data[i], preferred_element_type=jnp.float32)

    tile = 16

    def products(x, row, lane, first):
        here = (pl.ds(row, tile), pl.ds(lane, LANES))
        there = (pl.ds(row + seg, tile), pl.ds(lane, LANES))
        g_real = [spec[(i, *here)] for i in range(segs)]
        g_imag = [spec[(i, *there)] for i in range(segs)]
        k_real = [kern[(x, r, *here)].astype(jnp.float32) for r in range(segs)]
        k_imag = [kern[(x, r, *there)].astype(jnp.float32) for r in range(segs)]
        if first:
            edge = lax.broadcasted_iota(jnp.int32, (tile, LANES), 0) == 0
        for j in range(segs):
            both = sum(g_real[i] * k_real[i - j] for i in range(j, segs))
            other = sum(g_imag[i] * k_imag[i - j] for i in range(j, segs))
            cross = sum(g_imag[i] * k_real[i - j] - g_real[i] * k_imag[i - j] for i in range(j, segs))
            if first:
                real = both + jnp.where(edge, 0.0, other)
                cross = jnp.where(edge, other, cross)
            else:
                real = both + other
            acc[(j, *here)] = real.astype(jnp.bfloat16)
            acc[(j, *there)] = cross.astype(jnp.bfloat16)

    for x in range(2):
        for lane in range(0, width, LANES):
            products(x, 0, lane, True)

            @pl.loop(1, seg // tile, unroll=seg // tile - 1)
            def _(t):
                products(x, pl.multiple_of(t * tile, tile), lane, False)

        for j in range(segs):
            value = jnp.dot(back[...], acc[j], preferred_element_type=jnp.float32).astype(jnp.bfloat16)
            for core in range(2):
                result[2 * j + core, x] = value[core * rows : (core + 1) * rows]
    me = 2 * spot.chip + spot.core
    for k in range(n):
        outs[k][...] = result[me ^ k]


def correlate(forward, back, kern, pieces):
    ks, flat = tuple(pieces), tuple(pieces.values())
    segs = len(flat)
    _, rows, width = flat[0].shape
    seg = 2 * rows
    n = 2 * segs
    out = array((2, rows, width))
    return call(
        functools.partial(correlate_kernel, ks),
        (forward, back, kern, *flat),
        [whole(forward), whole(back), VMEM] + [whole(p) for p in flat],
        [out] * n,
        [whole(out)] * n,
        "correlate",
        [
            pltpu.VMEM((segs, seg, width), jnp.bfloat16),
            pltpu.VMEM((segs, 2 * seg, width), jnp.float32),
            pltpu.VMEM((segs, 2 * seg, width), jnp.bfloat16),
            pltpu.VMEM((n, *out.shape), jnp.bfloat16),
        ],
    )


def finish_kernel(ks, factor, fetch_branches, spot, *refs):
    n = len(ks)
    if fetch_branches:
        (key, value, *pieces), refs = refs[: 2 + n], refs[2 + n :]
        branches, *outs, key_o, value_o, filter_o, in_sem, out_sem = refs
    else:
        (branches, *pieces), refs = refs[: 1 + n], refs[1 + n :]
        *outs, key_o, value_o, filter_o, in_sem, out_sem = refs
    width = pieces[0].shape[2]
    me = 2 * spot.chip + spot.core
    loads = []
    if fetch_branches:
        loads.append(pltpu.make_async_copy(key, branches.at[0], in_sem.at[n]))
        loads.append(pltpu.make_async_copy(value, branches.at[1], in_sem.at[n + 1]))
    for copy in loads:
        copy.start()
    for copy in loads:
        copy.wait()
    stores = []
    for i, k in enumerate(ks):
        here = (slice(None), pl.ds(pl.multiple_of((me ^ k) * width, width), width))
        conv_grad = pieces[i][0].astype(jnp.float32)
        key_o[i] = (conv_grad * branches[(1, *here)].astype(jnp.float32)).astype(jnp.bfloat16)
        value_o[i] = (conv_grad * branches[(0, *here)].astype(jnp.float32)).astype(jnp.bfloat16)
        filter_o[i] = pieces[i][1].astype(jnp.float32) * factor
        for o, (src, dst) in enumerate(zip((key_o, value_o, filter_o), outs)):
            stores.append(pltpu.make_async_copy(src.at[i], dst.at[here], out_sem.at[o, i]))
            stores[-1].start()
    for copy in stores:
        copy.wait()


def finish(ks, pieces, factor, key=None, value=None, branches=None, grads=None):
    begin = branches is None
    n = len(ks)
    rows, width = pieces[0].shape[1:]
    scratch = [
        pltpu.VMEM((n, rows, width), jnp.bfloat16),
        pltpu.VMEM((n, rows, width), jnp.bfloat16),
        pltpu.VMEM((n, rows, width), jnp.float32),
        pltpu.SemaphoreType.DMA((n + 2,)),
        pltpu.SemaphoreType.DMA((3, n)),
    ]
    kernel = functools.partial(finish_kernel, ks, factor, begin)
    if begin:
        both = pltpu.VMEM((2, *key.shape), key.dtype)
        outs = [both, array(key.shape), array(key.shape), array(key.shape, jnp.float32)]
        args = (key, value, *pieces)
        return call(kernel, args, [ANY, ANY, *[VMEM] * n], outs, [VMEM, *[ANY] * 3], "finish", scratch)
    args = (branches, *pieces)
    return call(kernel, args, [VMEM] * (1 + n), [], [], "finish", scratch, update=grads)


def hold(arrays, after):
    return call(lambda spot: None, (), [], [], [], "hold", carry=arrays, after=after)


def swap(x, k, n):
    return lax.ppermute(x, "seq", [(i, i ^ k) for i in range(n)]) if k else x


def fast_shards(grad_out, out_weight, query_gate, key_branch, value_branch, filter_taps):
    n = lax.axis_size("seq")
    planes = lax.axis_size("ch")
    rows = grad_out.shape[0]
    chips = n // 2
    factor = 1.0 / math.sqrt(rows * n)
    forward, back = (jnp.asarray(t) for t in half_tables(2 * rows))
    outer = [(i, i ^ 1) for i in range(planes)]
    inner = []
    for s in range(n):
        inner += [(s * planes + 1, s * planes + 2), (s * planes + 2, s * planes + 1)]
        inner += [(s * planes + z, (s ^ 1) * planes + z) for z in (0, planes - 1)]

    def send_outer(x):
        return lax.ppermute(x, "ch", outer)

    def send_inner(x):
        return lax.ppermute(x, ("seq", "ch"), inner)

    def other(x):
        return swap(x, 1, n)

    outer_0, inner_0, others = send_outer(grad_out), send_inner(grad_out), other(grad_out)
    mine, *packed, packed_mark = pack(query_gate, key_branch, value_branch, filter_taps, chips)
    gates, taps_input, (merged,) = merge(mine, [other(x) for x in packed], after=[packed_mark])
    taps_input = [swap(x, 2 * k, n) for k, x in enumerate(taps_input)]
    outer_1, inner_1 = send_outer(inner_0), send_inner(outer_0)
    held, loaded = load(out_weight, chips, after=[merged])
    kern, tapped = tap_kernels(forward, taps_input, after=[loaded])
    outer_1, inner_1, gone = hold([outer_1, inner_1], after=[tapped])
    outer_2 = send_outer(inner_1)
    total, first = mix(0, [[grad_out], [others]], held, None, after=[gone])
    total, outer_1, second = mix(1, [[outer_0], [other(outer_0)]], held, total, carry=[outer_1], after=[first])
    blocks = [[outer_1, inner_0], [other(outer_1), other(inner_0)]]
    total, _ = mix(2, blocks, held, total, after=[second])
    gated = mix_gate([[outer_2, inner_1], [other(outer_2), other(inner_1)]], held, total, gates)[:chips]
    order = [0, *sorted(range(1, chips), key=lambda k: (-k.bit_count(), -k))]
    gated = {k: swap(gated[k], 2 * k, n) for k in order}

    results = correlate(forward, back, kern, gated)[:n]
    order = sorted(range(n), key=lambda k: ((k // 2).bit_count(), k % 2, k))
    results = {k: swap(results[k], k, n) for k in order}
    near, far = order[: n // 2], order[n // 2 :]
    branches, *grads, _ = finish(near, [results[k] for k in near], factor, key=key_branch, value=value_branch)
    return tuple(finish(far, [results[k] for k in far], factor, branches=branches, grads=grads)[:3])


def solution(mesh):
    specs = dict(
        mesh=mesh,
        in_specs=(
            P("seq", "ch"),
            P("ch", None),
            P("seq", "ch"),
            P("seq", "ch"),
            P("seq", "ch"),
            P("seq", "ch"),
        ),
        out_specs=(P("seq", "ch"), P("seq", "ch"), P("seq", "ch")),
        check_vma=False,
    )
    n, planes = mesh.shape["seq"], mesh.shape["ch"]

    def step(*arrays):
        whole_tiles = arrays[1].shape[0] // planes % (n * LANES) == 0
        fits = whole_tiles and planes == 4 and n & (n - 1) == 0
        return jax.shard_map(fast_shards if fits else shards, **specs)(*arrays)

    return step
```
